128 devices in a mesh: rec: 4 (over x_hi, core), tm: 32 (over x_lo, y, z).
Axes of the slice: x: 4 (x_hi: 2, x_lo: 2; x = x_hi * 2 + x_lo), y: 4, z: 4, core: 2. Of those that a mesh axis runs over, the one named last changes fastest.
Arguments:
- frames: bfloat16 [4, 16384, 1024], P('rec', 'tm'), may hold values from -6 to 6
- cotangent: bfloat16 [4, 16384, 1024], P('rec', 'tm'), may hold values from -6 to 6
- lengths: int32 [4], P('rec'), may hold values from 2048 to 16384, as said below
- w_query: bfloat16 [1024, 1024], replicated, may hold values from -1 to 1
- w_key: bfloat16 [1024, 1024], replicated, may hold values from -4 to 4
- w_value: bfloat16 [1024, 1024], replicated, may hold values from -0.1875 to 0.1875
- w_out: bfloat16 [1024, 1024], replicated, may hold values from -0.1875 to 0.1875
Outputs:
- grad_frames: bfloat16 [4, 16384, 1024], P('rec', 'tm')
- grad_projections: float32 [1024, 3072], P(('rec', 'tm'))
The draws below stay inside these ranges and needn't reach their ends.
Inputs may be any that keep to these rules, and one draw needn't show every extreme that they name: `lengths`: one recording is whole in every draw.
All inputs are finite; a program needn't handle non-finite values.
Results may differ from the reference program's by a relative error of at most 0.019.
Values may be sent and summed in bfloat16 or wider, within the bound.
No kernel may reach another device: no remote copies, remote signals or barrier semaphores. Data moves between devices by JAX's collectives and lax.ppermute only.
A program may use at most 128 MiB of HBM per device.

```python
import jax
import jax.numpy as jnp
from jax import lax

D = 1024
HEADS = 8
WIN = 128
HDIM = 128
LENGTH = 16384
RECS = 4


def shared_base(key):
    base = jax.random.normal(key, (D, D), jnp.float32) * D ** (-0.5)
    return jnp.clip(base, -6.0 * D ** (-0.5), 6.0 * D ** (-0.5))


def draw_w_query(key, part):
    base = shared_base(key)
    return jnp.clip(base, -1.0, 1.0).astype(jnp.bfloat16)


def draw_w_key(key, part):
    key = jax.random.fold_in(key, 7)
    result = jax.random.normal(key, (D, D), jnp.float32) * D ** (-0.5)
    return jnp.clip(result, -4.0, 4.0).astype(jnp.bfloat16)


def draw_frames(key, part):
    key = jax.random.fold_in(key, 3)
    noise_key = jax.random.fold_in(key, 0)
    result = jax.random.normal(noise_key, (RECS, LENGTH, D), jnp.float32)
    return jnp.clip(result, -6.0, 6.0).astype(jnp.bfloat16)


def draw_lengths(key, part):
    key = jax.random.fold_in(key, 11)
    length_key, whole_key = jax.random.split(key)
    drawn = jax.random.randint(length_key, (RECS,), LENGTH // 8, LENGTH + 1, jnp.int32)
    whole = jax.random.randint(whole_key, (), 0, RECS, jnp.int32)
    return drawn.at[whole].set(LENGTH).astype(jnp.int32)


def block_levels(key, dims, cuts, smallest, largest):
    factor_of, own = 1.0, jax.random.fold_in(key, 6)
    for dim, shards_of in cuts:
        steps = jnp.exp(jax.random.uniform(jax.random.fold_in(own, dim), (shards_of,), jnp.float32, smallest / len(cuts), largest / len(cuts)))
        factor_of = factor_of * jnp.repeat(steps, dims[dim] // shards_of).reshape([-1 if axis == dim else 1 for axis in range(len(dims))])
    return factor_of


def bell_draw(stream_key, dims, deviation, reach, shards=(), kind=jnp.bfloat16):
    array = jax.random.normal(stream_key, dims, jnp.float32) * deviation
    if len(shards) > 0:
        array = block_levels(stream_key, dims, shards, -0.22, 0.18) * array
    return jnp.clip(array, min=-reach, max=reach).astype(kind)


def setup_inputs(seed: int = 0) -> dict:
    arg_keys = jax.random.split(jax.random.key(seed), 8)
    return {
        "frames": draw_frames(jax.random.fold_in(arg_keys[7], 71), 0),
        "cotangent": bell_draw(arg_keys[1], (RECS, LENGTH, D), 1.0, 6.0, ((0, 4), (1, 32))),
        "lengths": draw_lengths(jax.random.fold_in(arg_keys[7], 71), 0),
        "w_query": draw_w_query(jax.random.fold_in(arg_keys[7], 71), 0),
        "w_key": draw_w_key(jax.random.fold_in(arg_keys[7], 71), 0),
        "w_value": bell_draw(arg_keys[5], (D, D), D ** -0.5, 0.1875),
        "w_out": bell_draw(arg_keys[6], (D, D), D ** -0.5, 0.1875),
    }


epsilon = 1e-05
masked_value = -1e+30

def normalize(frame_rows):
    values = frame_rows.astype(jnp.float32)
    center = values - lax.optimization_barrier(jnp.mean(values, -1, keepdims=True))
    inverse = lax.rsqrt(lax.optimization_barrier(jnp.mean(center * center, -1, keepdims=True)) + epsilon)
    return (center * inverse, inverse)

def attend(q_rows, k_rows, v_rows, d_rows, q_pos, k_pos, length):
    count = q_rows.shape[0]
    keys_count = k_rows.shape[0]
    q_heads = q_rows.reshape(count, HEADS, -1).astype(jnp.float32)
    k_heads = k_rows.reshape(keys_count, HEADS, -1).astype(jnp.float32)
    v_heads = v_rows.reshape(keys_count, HEADS, -1).astype(jnp.float32)
    d_heads = d_rows.reshape(count, HEADS, -1).astype(jnp.float32)
    scale = HDIM ** (-0.5)
    scores = jnp.einsum('qhd,khd->hqk', q_heads, k_heads) * scale
    allowed = (jnp.abs(q_pos[:, None] - k_pos[None, :]) <= WIN) & (k_pos[None, :] >= 0) & (k_pos[None, :] < length)
    scores = jnp.where(allowed[None], scores, masked_value)
    row_max = lax.optimization_barrier(jnp.max(scores, 2, keepdims=True))
    expo = jnp.exp(scores - row_max)
    prob = expo / lax.optimization_barrier(jnp.sum(expo, 2, keepdims=True))
    prob_b = prob.astype(jnp.bfloat16)
    mixed = jnp.einsum('hqk,khd->qhd', prob_b.astype(jnp.float32), v_heads).astype(jnp.bfloat16)
    d_prob = jnp.einsum('qhd,khd->hqk', d_heads, v_heads)
    row_delta = lax.optimization_barrier(jnp.sum(d_heads * mixed.astype(jnp.float32), 2)).T
    d_scores = (prob * (d_prob - row_delta[:, :, None]) * scale).astype(jnp.bfloat16)
    grad_q = jnp.einsum('hqk,khd->qhd', d_scores.astype(jnp.float32), k_heads).astype(jnp.bfloat16)
    grad_k = jnp.einsum('hqk,qhd->khd', d_scores.astype(jnp.float32), q_heads)
    grad_v = jnp.einsum('hqk,qhd->khd', prob_b.astype(jnp.float32), d_heads)
    return (mixed.reshape(count, -1), grad_q.reshape(count, -1), grad_k.reshape(keys_count, -1), grad_v.reshape(keys_count, -1))

def one_recording(frame_rows, grad_rows, length, w_query, w_key, w_value, w_out):
    normed, inverse = normalize(frame_rows)
    hidden = normed.astype(jnp.bfloat16)
    query = jnp.dot(hidden, w_query, preferred_element_type=jnp.float32).astype(jnp.bfloat16)
    keys = jnp.dot(hidden, w_key, preferred_element_type=jnp.float32).astype(jnp.bfloat16)
    values = jnp.dot(hidden, w_value, preferred_element_type=jnp.float32).astype(jnp.bfloat16)
    position = jnp.arange(LENGTH, dtype=jnp.int32)
    masked = jnp.where((position < length)[:, None], grad_rows, jnp.zeros_like(grad_rows))
    d_mixed = jnp.dot(masked, w_out.T, preferred_element_type=jnp.float32).astype(jnp.bfloat16)
    border = jnp.zeros((WIN, D), keys.dtype)
    keys_padded = jnp.concatenate([border, keys, border], 0)
    values_padded = jnp.concatenate([border, values, border], 0)
    height = min(512, LENGTH)
    blocks = LENGTH // height

    def step(carry, block_index):
        key_acc, value_acc = carry
        anchor = (block_index * height).astype(jnp.int32)
        q_rows = lax.dynamic_slice_in_dim(query, anchor, height, 0)
        d_rows = lax.dynamic_slice_in_dim(d_mixed, anchor, height, 0)
        k_rows = lax.dynamic_slice_in_dim(keys_padded, anchor, height + 2 * WIN, 0)
        v_rows = lax.dynamic_slice_in_dim(values_padded, anchor, height + 2 * WIN, 0)
        q_pos = anchor + jnp.arange(height, dtype=jnp.int32)
        k_pos = anchor - WIN + jnp.arange(height + 2 * WIN, dtype=jnp.int32)
        mixed, grad_q, grad_k, grad_v = attend(q_rows, k_rows, v_rows, d_rows, q_pos, k_pos, length)
        key_old = lax.dynamic_slice_in_dim(key_acc, anchor, height + 2 * WIN, 0)
        value_old = lax.dynamic_slice_in_dim(value_acc, anchor, height + 2 * WIN, 0)
        key_acc = lax.dynamic_update_slice_in_dim(key_acc, key_old + grad_k, anchor, 0)
        value_acc = lax.dynamic_update_slice_in_dim(value_acc, value_old + grad_v, anchor, 0)
        return ((key_acc, value_acc), (mixed, grad_q))
    zeros_start = jnp.zeros((LENGTH + 2 * WIN, D), jnp.float32)
    (key_acc, value_acc), (mixed_all, grad_q_all) = lax.scan(step, (zeros_start, zeros_start), jnp.arange(blocks, dtype=jnp.int32))
    grad_query = grad_q_all.reshape(LENGTH, D)
    grad_key = key_acc[WIN:WIN + LENGTH].astype(jnp.bfloat16)
    grad_value = value_acc[WIN:WIN + LENGTH].astype(jnp.bfloat16)
    d_hidden = jnp.dot(grad_query, w_query.T, preferred_element_type=jnp.float32) + jnp.dot(grad_key, w_key.T, preferred_element_type=jnp.float32) + jnp.dot(grad_value, w_value.T, preferred_element_type=jnp.float32)
    mean_grad = lax.optimization_barrier(jnp.mean(d_hidden, -1, keepdims=True))
    mean_cross = lax.optimization_barrier(jnp.mean(d_hidden * normed, -1, keepdims=True))
    grad_frames = (grad_rows.astype(jnp.float32) + inverse * (d_hidden - mean_grad - normed * mean_cross)).astype(jnp.bfloat16)
    weight_grads = jnp.concatenate([jnp.dot(hidden.T, grad_query, preferred_element_type=jnp.float32), jnp.dot(hidden.T, grad_key, preferred_element_type=jnp.float32), jnp.dot(hidden.T, grad_value, preferred_element_type=jnp.float32)], 1)
    return (grad_frames, weight_grads)

def reference(frames, cotangent, lengths, w_query, w_key, w_value, w_out):
    grad_list = []
    weight_total = jnp.zeros((D, 3 * D), jnp.float32)
    for record in range(RECS):
        grad_frames, weight_grads = one_recording(frames[record], cotangent[record], lengths[record], w_query, w_key, w_value, w_out)
        grad_list.append(grad_frames)
        weight_total = weight_total + weight_grads
    return (jnp.stack(grad_list), weight_total)
```

```python
import jax
import jax.numpy as jnp
from jax import lax
from jax.sharding import PartitionSpec as P

HEADS = 8
WIN = 128


AXES = ("rec", "tm")
CORE = 32
NEAR = ((16, 4, 1), (80, 12, 3))


def order_of(core):
    return NEAR[core] + NEAR[1 - core]


def exchange(value, masks):
    count = lax.axis_size(AXES)
    pairs = [(i, i ^ masks[(i // CORE) % 2]) for i in range(count)]
    return lax.ppermute(value, AXES, pairs)


def row_targets(me):
    row = jnp.arange(1024, dtype=jnp.int32)
    far = (row >> 9) & 1
    core = ((me // CORE) % 2) ^ far
    target = me ^ (far * CORE)
    for bit in range(6):
        mask = jnp.where(core == 0, order_of(0)[bit], order_of(1)[bit])
        target = target ^ (((row >> (8 - bit)) & 1) * mask)
    return target * 8 + (row & 7)


def halves(value, dim):
    return lax.index_in_dim(value, 0, dim, False), lax.index_in_dim(value, 1, dim, False)


def add(a, b):
    return (a.astype(jnp.float32) + b.astype(jnp.float32)).astype(jnp.bfloat16)


def scatter_sum(parts):
    masks = list(zip(order_of(0), order_of(1)))
    values = [part.reshape(2, 2, 2, 2, 2, 2, 8, -1) for part in parts]
    left = [[0, 1, 2] for _ in values]
    for step in range(3):
        sent = []
        for part in range(3):
            bit = (part + step) % 3
            keep, send = halves(values[part], left[part].index(bit))
            left[part].remove(bit)
            sent.append((keep, exchange(send, masks[bit])))
        values = [add(keep, got) for keep, got in sent]
    value = jnp.concatenate(values, -1)
    for bit in range(3, 6):
        keep, send = value[0], value[1]
        got = exchange(send, masks[bit])
        value = add(keep, got) if bit < 5 else keep.astype(jnp.float32) + got.astype(jnp.float32)
    return value


epsilon = 1e-05
masked_value = -1e30


def with_halo(block, sides, width):
    for axis, dim in sides:
        count = lax.axis_size(axis)
        forward = [(i, i + 1) for i in range(count - 1)]
        backward = [(target, source) for source, target in forward]
        low = lax.ppermute(
            lax.slice_in_dim(block, block.shape[dim] - width, None, axis=dim), axis, forward
        )
        high = lax.ppermute(lax.slice_in_dim(block, 0, width, axis=dim), axis, backward)
        block = jnp.concatenate([low, block, high], axis=dim)
    return block


def shifted(value, axis, steps):
    count = lax.axis_size(axis)
    first, last = (max(0, -steps), min(count, count - steps))
    return lax.ppermute(value, axis, [(source, source + steps) for source in range(first, last)])


def normalize(frame_rows):
    values = frame_rows.astype(jnp.float32)
    center = values - jnp.mean(values, -1, keepdims=True)
    inverse = lax.rsqrt(jnp.mean(center * center, -1, keepdims=True) + epsilon)
    return (center * inverse, inverse)


def masked_scores(q_heads, k_heads, q_pos, k_pos, length):
    scale = q_heads.shape[2] ** (-0.5)
    scores = (
        jnp.einsum("qhd,khd->hqk", q_heads, k_heads, preferred_element_type=jnp.float32) * scale
    )
    allowed = (
        (jnp.abs(q_pos[:, None] - k_pos[None, :]) <= WIN)
        & (k_pos[None, :] >= 0)
        & (k_pos[None, :] < length)
    )
    return (jnp.where(allowed[None], scores, masked_value), scale)


def attend(q_rows, k_rows, v_rows, d_rows, q_pos, k_pos, length):
    count = q_rows.shape[0]
    keys_count = k_rows.shape[0]
    q_heads = q_rows.reshape(count, HEADS, -1)
    k_heads = k_rows.reshape(keys_count, HEADS, -1)
    v_heads = v_rows.reshape(keys_count, HEADS, -1)
    d_heads = d_rows.reshape(count, HEADS, -1)
    scores, scale = masked_scores(q_heads, k_heads, q_pos, k_pos, length)
    row_max = jnp.max(scores, 2)
    expo = jnp.exp(scores - row_max[:, :, None])
    row_sum = jnp.sum(expo, 2)
    prob = expo / row_sum[:, :, None]
    prob_b = prob.astype(jnp.bfloat16)
    mixed = jnp.einsum("hqk,khd->qhd", prob_b, v_heads, preferred_element_type=jnp.float32).astype(
        jnp.bfloat16
    )
    d_prob = jnp.einsum("qhd,khd->hqk", d_heads, v_heads, preferred_element_type=jnp.float32)
    row_delta = jnp.sum(d_heads.astype(jnp.float32) * mixed.astype(jnp.float32), 2).T
    d_scores = (prob * (d_prob - row_delta[:, :, None]) * scale).astype(jnp.bfloat16)
    grad_q = jnp.einsum(
        "hqk,khd->qhd", d_scores, k_heads, preferred_element_type=jnp.float32
    ).astype(jnp.bfloat16)
    grad_k = jnp.einsum("hqk,qhd->khd", d_scores, q_heads, preferred_element_type=jnp.float32)
    grad_v = jnp.einsum("hqk,qhd->khd", prob_b, d_heads, preferred_element_type=jnp.float32)
    return (
        grad_q.reshape(count, -1),
        grad_k.reshape(keys_count, -1),
        grad_v.reshape(keys_count, -1),
        row_max,
        row_sum,
        row_delta,
    )


def shards(frames, cotangent, lengths, w_query, w_key, w_value, w_out):
    frame_rows = frames[0]
    grad_rows = cotangent[0]
    length = lengths[0]
    height = frame_rows.shape[0]
    width = frame_rows.shape[1]
    anchor = lax.axis_index("tm") * height
    position = anchor + jnp.arange(height, dtype=jnp.int32)
    normed, inverse = normalize(frame_rows)
    hidden = normed.astype(jnp.bfloat16)
    query = jnp.dot(hidden, w_query, preferred_element_type=jnp.float32).astype(jnp.bfloat16)
    keys = jnp.dot(hidden, w_key, preferred_element_type=jnp.float32).astype(jnp.bfloat16)
    values = jnp.dot(hidden, w_value, preferred_element_type=jnp.float32).astype(jnp.bfloat16)
    masked = jnp.where((position < length)[:, None], grad_rows, jnp.zeros_like(grad_rows))
    d_mixed = jnp.einsum("tg,fg->tf", masked, w_out, preferred_element_type=jnp.float32).astype(
        jnp.bfloat16
    )
    padded = with_halo(jnp.stack([keys, values]), (("tm", 1),), WIN)
    block_rows = min(512, height)
    key_sum = jnp.zeros((height + 2 * WIN, width), jnp.float32)
    value_sum = jnp.zeros((height + 2 * WIN, width), jnp.float32)
    query_parts, max_parts, sum_parts, delta_parts = ([], [], [], [])
    span_end = block_rows + 2 * WIN
    k_pos = anchor - WIN + 0 + jnp.arange(block_rows + 2 * WIN, dtype=jnp.int32)
    grad_q, grad_k, grad_v, row_max, row_sum, row_delta = attend(
        query, padded[0, 0:span_end], padded[1, 0:span_end], d_mixed, position, k_pos, length
    )
    key_sum = key_sum.at[0:span_end].add(grad_k)
    value_sum = value_sum.at[0:span_end].add(grad_v)
    query_parts.append(grad_q)
    max_parts.append(row_max)
    sum_parts.append(row_sum)
    delta_parts.append(row_delta)
    grad_query = query_parts[0]
    key_own = key_sum[WIN : WIN + height]
    value_own = value_sum[WIN : WIN + height]
    toward_left = jnp.stack([key_sum[:WIN], value_sum[:WIN]])
    toward_right = jnp.stack([key_sum[height + WIN :], value_sum[height + WIN :]])
    from_right = shifted(toward_left.astype(jnp.bfloat16), "tm", -1).astype(toward_left.dtype)
    from_left = shifted(toward_right.astype(jnp.bfloat16), "tm", 1).astype(toward_right.dtype)
    key_own = key_own.at[height - WIN :].add(from_right[0]).at[:WIN].add(from_left[0])
    value_own = value_own.at[height - WIN :].add(from_right[1]).at[:WIN].add(from_left[1])
    grad_key = key_own.astype(jnp.bfloat16)
    grad_value = value_own.astype(jnp.bfloat16)
    d_hidden = (
        jnp.einsum("tg,fg->tf", grad_query, w_query, preferred_element_type=jnp.float32)
        + jnp.einsum("tg,fg->tf", grad_key, w_key, preferred_element_type=jnp.float32)
        + jnp.einsum("tg,fg->tf", grad_value, w_value, preferred_element_type=jnp.float32)
    )
    mean_grad = jnp.mean(d_hidden, -1, keepdims=True)
    mean_cross = jnp.mean(d_hidden * normed, -1, keepdims=True)
    grad_frames = (
        grad_rows.astype(jnp.float32) + inverse * (d_hidden - mean_grad - normed * mean_cross)
    ).astype(jnp.bfloat16)
    me = lax.axis_index(AXES)
    targets = row_targets(me)
    spread = (targets[None, :] == jnp.arange(width, dtype=jnp.int32)[:, None]).astype(jnp.bfloat16)
    ordered = jnp.dot(hidden, spread, preferred_element_type=jnp.float32).astype(jnp.bfloat16)
    projected = jnp.concatenate([grad_query, grad_key, grad_value], 1)
    partial = jnp.einsum("tf,tg->fg", ordered, projected, preferred_element_type=jnp.float32).astype(
        jnp.bfloat16
    )
    got = exchange(partial[512:], (CORE, CORE))
    own = add(partial[:512], got)
    weight_part = scatter_sum([own[:, :1024], own[:, 1024:2048], own[:, 2048:]])
    return (grad_frames[None], weight_part)


def solution(mesh):
    placed = (P("rec", "tm", None), P("rec", "tm", None), P("rec"), P(), P(), P(), P())
    return jax.shard_map(
        shards,
        mesh=mesh,
        in_specs=placed,
        out_specs=(P("rec", "tm", None), P(("rec", "tm"), None)),
        check_vma=False,
    )
```

```python
import functools
import math

import jax
import jax.numpy as jnp
from jax import lax
from jax.experimental import pallas as pl
from jax.experimental.pallas import tpu as pltpu
from jax.sharding import PartitionSpec as P

HEADS = 8
WIN = 128
HDIM = 128
ROWS = 512
D = 1024
PAIR = 2 * HDIM
STEPS = HEADS // 2
epsilon = 1e-05
masked_value = -1e30
F32 = jnp.float32
BF16 = jnp.bfloat16

AXES = ("rec", "tm")
CORE = 32
NEAR = ((16, 4, 1), (80, 12, 3))


def order_of(core):
    return NEAR[core] + NEAR[1 - core]


def exchange(value, masks):
    count = lax.axis_size(AXES)
    pairs = [(i, i ^ masks[(i // CORE) % 2]) for i in range(count)]
    return lax.ppermute(value, AXES, pairs)


def coordinates(device, core):
    high = [(device >> bit) & 1 for bit in (6, 3, 1)]
    low = [(device >> bit) & 1 for bit in (4, 2, 0)]
    return high if core == 0 else [a ^ b for a, b in zip(high, low)]


def row_targets(me):
    row = jnp.arange(1024, dtype=jnp.int32)
    far = (row >> 9) & 1
    core = ((me // CORE) % 2) ^ far
    target = me ^ (far * CORE)
    for bit in range(6):
        mask = jnp.where(core == 0, order_of(0)[bit], order_of(1)[bit])
        move = (row >> (8 - bit)) & 1
        if bit >= 3:
            move = move ^ jnp.where(core == 0, coordinates(me, 0)[bit - 3], coordinates(me, 1)[bit - 3])
        target = target ^ (move * mask)
    return target * 8 + (row & 7)


def last_groups():
    groups = []
    for device in range(128):
        core = (device // CORE) % 2
        if not any(coordinates(device, core)):
            one, two, three = order_of(core)[3:]
            groups.append([device ^ (a * one) ^ (b * two) ^ (c * three) for a in (0, 1) for b in (0, 1) for c in (0, 1)])
    return groups


def halves(value, dim):
    return lax.index_in_dim(value, 0, dim, False), lax.index_in_dim(value, 1, dim, False)


def add(a, b):
    return (a.astype(jnp.float32) + b.astype(jnp.float32)).astype(jnp.bfloat16)


def scatter_sum(parts, beside):
    masks = list(zip(order_of(0), order_of(1)))
    values = [part.reshape(2, 2, 2, 8, 8, -1) for part in parts]
    left = [[0, 1, 2] for _ in values]
    other = None
    for step in range(3):
        sent = []
        for part in range(3):
            bit = (part + step) % 3
            keep, send = halves(values[part], left[part].index(bit))
            left[part].remove(bit)
            sent.append((keep, exchange(send, masks[bit])))
        if step < len(beside):
            other = beside[step](values[0], other)
        values = [add(keep, got) for keep, got in sent]
        if step < len(beside):
            *values, other = lax.optimization_barrier((*values, other))
    value = jnp.concatenate(values, -1)
    got = lax.all_to_all(value, AXES, 0, 0, axis_index_groups=last_groups(), tiled=True)
    return jnp.sum(got.astype(jnp.float32), 0), other


def dot(a, b):
    return lax.dot_general(a, b, (((1,), (0,)), ((), ())), preferred_element_type=F32)


def dot_nt(a, b):
    return lax.dot_general(a, b, (((1,), (1,)), ((), ())), preferred_element_type=F32)


def dot_tn(a, b):
    return lax.dot_general(a, b, (((0,), (0,)), ((), ())), preferred_element_type=F32)


def normalize(rows):
    values = rows.astype(F32)
    center = values - jnp.mean(values, -1, keepdims=True)
    inverse = lax.rsqrt(jnp.mean(center * center, -1, keepdims=True) + epsilon)
    return center * inverse, inverse


def call(body, outs, ins, in_specs, out_specs, scratch, macs, steps=STEPS, room=30):
    size = sum(math.prod(x.shape) * x.dtype.itemsize for x in (*ins, *jax.tree.leaves(outs)))
    return pl.pallas_call(
        body,
        out_shape=outs,
        grid=(steps,),
        in_specs=in_specs,
        out_specs=out_specs,
        scratch_shapes=scratch,
        compiler_params=pltpu.CompilerParams(vmem_limit_bytes=room * 2**20),
        cost_estimate=pl.CostEstimate(flops=2 * macs, bytes_accessed=size, transcendentals=0),
    )(*ins)


def whole(*shape):
    return pl.BlockSpec(shape, lambda j: (0,) * len(shape))


def columns(rows):
    return pl.BlockSpec((rows, PAIR), lambda j: (0, j))


SCALAR = pl.BlockSpec(memory_space=pltpu.SMEM)


def one_hot(target):
    lane = lax.broadcasted_iota(jnp.int32, (target.shape[0], D), 1)
    return jnp.where(lane == target, 1.0, 0.0).astype(BF16)


def front_body(place, target, frames, grads, w_query, w_key, w_value, w_out, ordered, query, keys, values, d_mixed, hidden, masked):
    @pl.when(pl.program_id(0) == 0)
    def _():
        hidden[...] = normalize(frames[...])[0].astype(BF16)
        row = lax.broadcasted_iota(jnp.int32, (ROWS, D), 0) + place[0]
        masked[...] = jnp.where(row < place[1], grads[...].astype(F32), 0.0).astype(BF16)

    rows = hidden[...]
    query[...] = dot(rows, w_query[...]).astype(BF16)
    keys[...] = dot(rows, w_key[...]).astype(BF16)
    values[...] = dot(rows, w_value[...]).astype(BF16)
    d_mixed[...] = dot_nt(masked[...], w_out[...]).astype(BF16)
    ordered[...] = dot_nt(one_hot(target[...]), rows).astype(BF16)


def front(place, target, frames, grads, w_query, w_key, w_value, w_out):
    wide = jax.ShapeDtypeStruct((ROWS, D), BF16)
    return call(
        front_body,
        [jax.ShapeDtypeStruct((D, ROWS), BF16), wide, wide, wide, wide],
        (place, target, frames, grads, w_query, w_key, w_value, w_out),
        [SCALAR, pl.BlockSpec((PAIR, 1), lambda j: (j, 0)), whole(ROWS, D), whole(ROWS, D)]
        + [columns(D)] * 3
        + [pl.BlockSpec((PAIR, D), lambda j: (j, 0))],
        [pl.BlockSpec((PAIR, ROWS), lambda j: (j, 0))] + [columns(ROWS)] * 4,
        [pltpu.VMEM((ROWS, D), BF16)] * 2,
        5 * ROWS * D * D,
        room=60,
    )


def attend_body(
    place, target, low, high, ordered, query, keys, values, d_mixed, w_key, w_value,
    grad_query, grad_key, grad_value, kept, sent, sides,
    ordered_border, hidden_border, key_value, key_t, pair, score_t, prob_t, border_grads, total,
):
    scale = HDIM ** (-0.5)
    blocks = ROWS // WIN
    row = lax.broadcasted_iota(jnp.int32, (WIN, WIN), 0)
    eye = jnp.where(lax.broadcasted_iota(jnp.int32, (WIN, WIN), 1) == row, 1.0, 0.0).astype(BF16)

    @pl.when(pl.program_id(0) == 0)
    def _():
        hidden_border[:WIN] = normalize(low[...])[0].astype(BF16)
        hidden_border[WIN:] = normalize(high[...])[0].astype(BF16)
        for part in range(4):
            rows = slice(part * PAIR, (part + 1) * PAIR)
            ordered_border[rows] = dot_nt(one_hot(target[rows]), hidden_border[...]).astype(BF16)
        for ref in (pair, score_t, prob_t):
            ref[...] = jnp.zeros_like(ref)
        total[...] = jnp.zeros_like(total)

    key_border = dot(hidden_border[...], w_key[...]).astype(BF16)
    value_border = dot(hidden_border[...], w_value[...]).astype(BF16)
    above = lax.broadcasted_iota(jnp.int32, (3 * WIN, WIN), 0)
    lane = lax.broadcasted_iota(jnp.int32, (1, WIN), 1)

    def lay_out(head):
        cols = slice(head * HDIM, (head + 1) * HDIM)
        for side, own, to in ((key_border, keys, slice(0, HDIM)), (value_border, values, slice(HDIM, PAIR))):
            key_value[head, :WIN, to] = side[:WIN, cols]
            key_value[head, WIN : WIN + ROWS, to] = own[:, cols]
            key_value[head, WIN + ROWS :, to] = side[WIN:, cols]
        key_t[head] = dot_nt(eye, key_value[head, :, :HDIM]).astype(BF16)
        for i in range(blocks):
            mine = slice(i * WIN, (i + 1) * WIN)
            pair[head, i * PAIR : i * PAIR + WIN, :HDIM] = query[mine, cols]
            pair[head, i * PAIR + WIN : (i + 1) * PAIR, HDIM:] = d_mixed[mine, cols]

    def products(head, i):
        return dot_nt(key_value[head, i * WIN : (i + 3) * WIN], pair[head, i * PAIR : (i + 1) * PAIR])

    def soften(head, i, both):
        mine = slice(i * WIN, (i + 1) * WIN)
        reach = slice(i * WIN, (i + 3) * WIN)
        first = (1 - i) * WIN - place[0]
        last = place[1] - place[0] + (1 - i) * WIN - 1
        allowed = (above >= jnp.maximum(lane, first)) & (above <= jnp.minimum(lane + 2 * WIN, last))
        scores = jnp.where(allowed, both[:, :WIN], masked_value)
        d_prob = both[:, WIN:]
        row_max = jnp.max(scores, 0, keepdims=True)
        expo = jnp.exp2((scores - row_max) * (scale * math.log2(math.e)))
        inverse_sum = 1.0 / jnp.sum(expo, 0, keepdims=True)
        row_delta = jnp.sum(expo * d_prob, 0, keepdims=True) * inverse_sum
        score_t[head, reach, mine] = (expo * (inverse_sum * scale) * (d_prob - row_delta)).astype(BF16)
        prob_t[head, reach, mine] = (expo * inverse_sum).astype(BF16)

    def query_grads(head, part):
        cols = slice(head * HDIM, (head + 1) * HDIM)
        mine = slice(part * PAIR, (part + 1) * PAIR)
        reach = slice(part * PAIR, part * PAIR + 2 * PAIR)
        grad_t = dot(key_t[head, :, reach], score_t[head, reach, mine]).astype(BF16)
        for half in (slice(0, WIN), slice(WIN, PAIR)):
            rows = slice(part * PAIR + half.start, part * PAIR + half.stop)
            grad_query[rows, cols] = dot_nt(eye, grad_t[:, half]).astype(BF16)

    def key_grads(head, part):
        cols = slice(head * HDIM, (head + 1) * HDIM)
        here = slice(part * PAIR, (part + 1) * PAIR)
        near = slice(max(0, part - 1) * PAIR, min(2, part + 1) * PAIR)
        g_key = dot(score_t[head, here, near], query[near, cols]).astype(BF16)
        g_value = dot(prob_t[head, here, near], d_mixed[near, cols]).astype(BF16)
        if part == 0:
            border_grads[0, :WIN, cols], border_grads[1, :WIN, cols] = g_key[:WIN], g_value[:WIN]
            grad_key[:WIN, cols], grad_value[:WIN, cols] = g_key[WIN:], g_value[WIN:]
        elif part == 1:
            grad_key[WIN : WIN + PAIR, cols], grad_value[WIN : WIN + PAIR, cols] = g_key, g_value
        else:
            grad_key[ROWS - WIN :, cols], grad_value[ROWS - WIN :, cols] = g_key[:WIN], g_value[:WIN]
            border_grads[0, WIN:, cols], border_grads[1, WIN:, cols] = g_key[WIN:], g_value[WIN:]

    lay_out(0)
    lay_out(1)
    first = [products(0, i) for i in range(blocks)]
    second = []
    for i in range(blocks):
        soften(0, i, first[i])
        second.append(products(1, i))
    jobs = [(query_grads, 0), (query_grads, 1), (key_grads, 0), (key_grads, 1), (key_grads, 2)]
    for i in range(blocks):
        soften(1, i, second[i])
        for job, part in jobs[i : i + 1] if i < 3 else jobs[3:]:
            job(0, part)
    for job, part in jobs:
        job(1, part)
    half = D // 2
    for out, rows in ((sent, slice(half, D)), (kept, slice(0, half))):
        out[0] = dot(ordered[rows], grad_query[...]).astype(BF16)
        out[1] = (dot(ordered[rows], grad_key[...]) + dot(ordered_border[rows], border_grads[0])).astype(BF16)
        out[2] = (dot(ordered[rows], grad_value[...]) + dot(ordered_border[rows], border_grads[1])).astype(BF16)
    total[...] += dot_nt(border_grads[0], w_key[...]) + dot_nt(border_grads[1], w_value[...])

    @pl.when(pl.program_id(0) == STEPS - 1)
    def _():
        sides[...] = total[...].astype(BF16)


def attend(place, target, low, high, ordered, query, keys, values, d_mixed, w_key, w_value):
    own = jax.ShapeDtypeStruct((ROWS, D), BF16)
    half = jax.ShapeDtypeStruct((3, D // 2, D), BF16)
    reach = ROWS + 2 * WIN
    return call(
        attend_body,
        [own] * 3 + [half] * 2 + [jax.ShapeDtypeStruct((2 * WIN, D), BF16)],
        (place, target, low, high, ordered, query, keys, values, d_mixed, w_key, w_value),
        [SCALAR, whole(D, 1), whole(WIN, D), whole(WIN, D), whole(D, ROWS)] + [columns(ROWS)] * 4 + [columns(D)] * 2,
        [columns(ROWS)] * 3 + [pl.BlockSpec((3, D // 2, PAIR), lambda j: (0, 0, j))] * 2 + [whole(2 * WIN, D)],
        [
            pltpu.VMEM((D, 2 * WIN), BF16),
            pltpu.VMEM((2 * WIN, D), BF16),
            pltpu.VMEM((2, reach, PAIR), BF16),
            pltpu.VMEM((2, HDIM, reach), BF16),
            pltpu.VMEM((2, 2 * ROWS, PAIR), BF16),
            pltpu.VMEM((2, reach, ROWS), BF16),
            pltpu.VMEM((2, reach, ROWS), BF16),
            pltpu.VMEM((2, 2 * WIN, PAIR), BF16),
            pltpu.VMEM((2 * WIN, D), F32),
        ],
        D * D * (ROWS * 3 + WIN * 12) + 10 * 4 * 3 * HEADS * WIN**3,
    )


def back_body(grad_query, grad_key, grad_value, w_query, w_key, w_value, total):
    part = dot_nt(grad_query[...], w_query[...]) + dot_nt(grad_key[...], w_key[...]) + dot_nt(grad_value[...], w_value[...])

    @pl.when(pl.program_id(0) == 0)
    def _():
        total[...] = part

    @pl.when(pl.program_id(0) > 0)
    def _():
        total[...] += part


def back(*ins):
    return call(
        back_body,
        jax.ShapeDtypeStruct((ROWS, D), F32),
        ins,
        [columns(ROWS)] * 3 + [columns(D)] * 3,
        whole(ROWS, D),
        [],
        3 * ROWS * D * D,
    )


def finish_body(frames, grads, d_hidden, near, out):
    normed, inverse = normalize(frames[...])
    part = pl.program_id(0)
    inner = jnp.logical_and(part > 0, part < STEPS - 1)
    d_rows = d_hidden[...] + jnp.where(inner, 0.0, near[...].astype(F32))
    mean_grad = jnp.mean(d_rows, -1, keepdims=True)
    mean_cross = jnp.mean(d_rows * normed, -1, keepdims=True)
    out[...] = (grads[...].astype(F32) + inverse * (d_rows - mean_grad - normed * mean_cross)).astype(BF16)


def finish(frames, grads, d_hidden, near):
    block = pl.BlockSpec((WIN, D), lambda j: (j, 0))
    return call(
        finish_body,
        jax.ShapeDtypeStruct((ROWS, D), BF16),
        (frames, grads, d_hidden, near),
        [block] * 3 + [pl.BlockSpec((WIN, D), lambda j: (j // (STEPS - 1), 0))],
        block,
        [],
        ROWS * D * 16,
    )


def swap_borders(first, last):
    count = lax.axis_size("tm")
    even = lax.axis_index("tm") % 2 == 0
    one = [(i, i ^ 1) for i in range(count)]
    two = [(i, i + 1 if i % 2 else i - 1) for i in range(1, count - 1)]
    a = lax.ppermute(jnp.where(even, last, first), "tm", one)
    b = lax.ppermute(jnp.where(even, first, last), "tm", two)
    return jnp.where(even, b, a), jnp.where(even, a, b)


def shards(frames, cotangent, lengths, w_query, w_key, w_value, w_out):
    rows, grads = frames[0], cotangent[0]
    low, high = swap_borders(rows[:WIN], rows[ROWS - WIN :])
    place = jnp.stack([lax.axis_index("tm") * ROWS, lengths[0]]).astype(jnp.int32)
    target = row_targets(lax.axis_index(AXES))[:, None]
    ordered, query, keys, values, d_mixed = front(place, target, rows, grads, w_query, w_key, w_value, w_out)
    grad_query, grad_key, grad_value, kept, sent, sides = attend(
        place, target, low, high, ordered, query, keys, values, d_mixed, w_key, w_value
    )
    got = exchange(sent, (CORE, CORE))
    from_low, from_high = swap_borders(sides[:WIN], sides[WIN:])
    own = add(kept, got)

    def first(after, _):
        query_now, _ = lax.optimization_barrier((grad_query, after))
        return back(query_now, grad_key, grad_value, w_query, w_key, w_value)

    def second(after, d_hidden):
        near, _ = lax.optimization_barrier((jnp.concatenate([from_low, from_high]), after))
        return finish(rows, grads, d_hidden, near)

    weight_part, grad_frames = scatter_sum([own[0], own[1], own[2]], (first, second))
    return (grad_frames[None], weight_part)


def solution(mesh):
    placed = (P("rec", "tm", None), P("rec", "tm", None), P("rec"), P(), P(), P(), P())
    return jax.shard_map(
        shards,
        mesh=mesh,
        in_specs=placed,
        out_specs=(P("rec", "tm", None), P(("rec", "tm"), None)),
        check_vma=False,
    )
```

```python
import functools
import math

import jax
import jax.numpy as jnp
from jax import lax
from jax.experimental import pallas as pl
from jax.experimental.pallas import tpu as pltpu
from jax.sharding import PartitionSpec as P

HEADS = 8
WIN = 128
HDIM = 128
ROWS = 512
D = 1024
PAIR = 2 * HDIM
STEPS = HEADS // 2
epsilon = 1e-05
masked_value = -1e30
F32 = jnp.float32
BF16 = jnp.bfloat16
ROOM = (30, 30, 30, 30)

AXES = ("rec", "tm")
CORE = 32
NEAR = ((16, 4, 1), (80, 12, 3))


def order_of(core):
    return NEAR[core] + NEAR[1 - core]


def exchange(value, masks):
    count = lax.axis_size(AXES)
    pairs = [(i, i ^ masks[(i // CORE) % 2]) for i in range(count)]
    return lax.ppermute(value, AXES, pairs)


def coordinates(device, core):
    high = [(device >> bit) & 1 for bit in (6, 3, 1)]
    low = [(device >> bit) & 1 for bit in (4, 2, 0)]
    return high if core == 0 else [a ^ b for a, b in zip(high, low)]


def block_targets():
    me = lax.axis_index(AXES)
    block = jnp.arange(128, dtype=jnp.int32)
    far = block >> 6
    core = ((me >> 5) & 1) ^ far
    target = me ^ (far * CORE)
    for bit in range(6):
        masks = order_of(0)[bit], order_of(1)[bit]
        move = (block >> (5 - bit)) & 1
        if bit >= 3:
            zero, one = coordinates(me, 0)[bit - 3], coordinates(me, 1)[bit - 3]
            move = move ^ (zero + core * (one - zero))
        target = target ^ (move * (masks[0] + core * (masks[1] - masks[0])))
    return target


def last_groups():
    groups = []
    for device in range(128):
        core = (device // CORE) % 2
        if not any(coordinates(device, core)):
            one, two, three = order_of(core)[3:]
            groups.append([device ^ (a * one) ^ (b * two) ^ (c * three) for a in (0, 1) for b in (0, 1) for c in (0, 1)])
    return groups


def halves(value, dim):
    return lax.index_in_dim(value, 0, dim, False), lax.index_in_dim(value, 1, dim, False)


def add(a, b):
    return (a.astype(jnp.float32) + b.astype(jnp.float32)).astype(jnp.bfloat16)


def scatter_sum(parts, beside):
    masks = list(zip(order_of(0), order_of(1)))
    values = [part.reshape(2, 2, 2, 8, 8, -1) for part in parts]
    left = [[0, 1, 2] for _ in values]
    other = None
    for step in range(3):
        sent = []
        for part in range(3):
            bit = (part + step) % 3
            keep, send = halves(values[part], left[part].index(bit))
            left[part].remove(bit)
            sent.append((keep, exchange(send, masks[bit])))
        other = beside[step](values[0], other)
        values = [add(keep, got) for keep, got in sent]
        if step > 0:
            values, other = lax.optimization_barrier((values, other))
    value = jnp.concatenate(values, -1)
    got = lax.all_to_all(value, AXES, 0, 0, axis_index_groups=last_groups(), tiled=True)
    return jnp.sum(got.astype(jnp.float32), 0), other


def dot(a, b):
    return lax.dot_general(a, b, (((1,), (0,)), ((), ())), preferred_element_type=F32)


def dot_nt(a, b):
    return lax.dot_general(a, b, (((1,), (1,)), ((), ())), preferred_element_type=F32)


def dot_tn(a, b):
    return lax.dot_general(a, b, (((0,), (0,)), ((), ())), preferred_element_type=F32)


def normalize(rows):
    values = rows.astype(F32)
    center = values - jnp.mean(values, -1, keepdims=True)
    inverse = lax.rsqrt(jnp.mean(center * center, -1, keepdims=True) + epsilon)
    return center * inverse, inverse


def call(body, outs, ins, in_specs, out_specs, scratch, macs, steps=STEPS, room=30):
    size = sum(math.prod(x.shape) * x.dtype.itemsize for x in (*ins, *jax.tree.leaves(outs)))
    return pl.pallas_call(
        body,
        out_shape=outs,
        grid=(steps,),
        in_specs=in_specs,
        out_specs=out_specs,
        scratch_shapes=scratch,
        compiler_params=pltpu.CompilerParams(vmem_limit_bytes=room * 2**20),
        cost_estimate=pl.CostEstimate(flops=2 * macs, bytes_accessed=size, transcendentals=0),
    )(*ins)


def whole(*shape):
    return pl.BlockSpec(shape, lambda j: (0,) * len(shape))


def columns(rows):
    return pl.BlockSpec((rows, PAIR), lambda j: (0, j))


SCALAR = pl.BlockSpec(memory_space=pltpu.SMEM)


def one_hot(target, first, blocks):
    lane = lax.broadcasted_iota(jnp.int32, (8, D), 1) - lax.broadcasted_iota(jnp.int32, (8, D), 0)
    rows = [jnp.where(lane == 8 * target[first + block], 1.0, 0.0) for block in range(blocks)]
    return jnp.concatenate(rows, 0).astype(BF16)


def here():
    return lax.axis_index("tm") * ROWS


def front_body(length, target, frames, grads, w_query, w_key, w_value, w_out, ordered, query, keys, values, d_mixed, hidden, masked):
    @pl.when(pl.program_id(0) == 0)
    def _():
        hidden[...] = normalize(frames[...])[0].astype(BF16)
        row = lax.broadcasted_iota(jnp.int32, (ROWS, D), 0) + here()
        masked[...] = jnp.where(row < length[0], grads[...].astype(F32), 0.0).astype(BF16)

    rows = hidden[...]
    d_mixed[...] = dot_nt(masked[...], w_out[...]).astype(BF16)
    query[...] = dot(rows, w_query[...]).astype(BF16)
    keys[...] = dot(rows, w_key[...]).astype(BF16)
    values[...] = dot(rows, w_value[...]).astype(BF16)
    ordered[...] = dot_nt(one_hot(target, pl.program_id(0) * (PAIR // 8), PAIR // 8), rows).astype(BF16)


def front(length, target, frames, grads, w_query, w_key, w_value, w_out):
    wide = jax.ShapeDtypeStruct((ROWS, D), BF16)
    return call(
        front_body,
        [jax.ShapeDtypeStruct((D, ROWS), BF16), wide, wide, wide, wide],
        (length, target, frames, grads, w_query, w_key, w_value, w_out),
        [SCALAR, SCALAR, whole(ROWS, D), whole(ROWS, D)] + [columns(D)] * 3 + [pl.BlockSpec((PAIR, D), lambda j: (j, 0))],
        [pl.BlockSpec((PAIR, ROWS), lambda j: (j, 0))] + [columns(ROWS)] * 4,
        [pltpu.VMEM((ROWS, D), BF16)] * 2,
        5 * ROWS * D * D,
        room=ROOM[0],
    )


def attend_body(
    length, target, low, high, ordered, query, keys, values, d_mixed, w_key, w_value,
    grad_query, grad_key, grad_value, border_grads, kept, sent,
    ordered_border, hidden_border, key_value, pair, score_t, prob_t,
):
    scale = HDIM ** (-0.5)
    blocks = ROWS // WIN

    @pl.when(pl.program_id(0) == 0)
    def _():
        hidden_border[:WIN] = normalize(low[...])[0].astype(BF16)
        hidden_border[WIN:] = normalize(high[...])[0].astype(BF16)
        for part in range(4):
            rows = slice(part * PAIR, (part + 1) * PAIR)
            ordered_border[rows] = dot_nt(one_hot(target, part * (PAIR // 8), PAIR // 8), hidden_border[...]).astype(BF16)
        for ref in (pair, score_t, prob_t):
            ref[...] = jnp.zeros_like(ref)

    key_border = dot(hidden_border[...], w_key[...]).astype(BF16)
    value_border = dot(hidden_border[...], w_value[...]).astype(BF16)
    above = lax.broadcasted_iota(jnp.int32, (3 * WIN, WIN), 0)
    lane = lax.broadcasted_iota(jnp.int32, (1, WIN), 1)

    def lay_out(head):
        cols = slice(head * HDIM, (head + 1) * HDIM)
        for side, own, to in ((key_border, keys, slice(0, HDIM)), (value_border, values, slice(HDIM, PAIR))):
            key_value[head, :WIN, to] = side[:WIN, cols]
            key_value[head, WIN : WIN + ROWS, to] = own[:, cols]
            key_value[head, WIN + ROWS :, to] = side[WIN:, cols]
        for i in range(blocks):
            mine = slice(i * WIN, (i + 1) * WIN)
            pair[head, i * PAIR : i * PAIR + WIN, :HDIM] = query[mine, cols]
            pair[head, i * PAIR + WIN : (i + 1) * PAIR, HDIM:] = d_mixed[mine, cols]

    def products(head, i):
        return dot_nt(key_value[head, i * WIN : (i + 3) * WIN], pair[head, i * PAIR : (i + 1) * PAIR])

    def soften(head, i, both):
        mine = slice(i * WIN, (i + 1) * WIN)
        reach = slice(i * WIN, (i + 3) * WIN)
        first = (1 - i) * WIN - here()
        last = length[0] - here() + (1 - i) * WIN - 1
        allowed = (above >= jnp.maximum(lane, first)) & (above <= jnp.minimum(lane + 2 * WIN, last))
        scores = jnp.where(allowed, both[:, :WIN], masked_value)
        d_prob = both[:, WIN:]
        row_max = jnp.max(scores, 0, keepdims=True)
        expo = jnp.exp2((scores - row_max) * (scale * math.log2(math.e)))
        inverse_sum = 1.0 / jnp.sum(expo, 0, keepdims=True)
        row_delta = jnp.sum(expo * d_prob, 0, keepdims=True) * inverse_sum
        score_t[head, reach, mine] = (expo * (inverse_sum * scale) * (d_prob - row_delta)).astype(BF16)
        prob_t[head, reach, mine] = (expo * inverse_sum).astype(BF16)

    def query_grads(head, part):
        cols = slice(head * HDIM, (head + 1) * HDIM)
        mine = slice(part * PAIR, (part + 1) * PAIR)
        reach = slice(part * PAIR, part * PAIR + 2 * PAIR)
        grad_query[mine, cols] = dot_tn(score_t[head, reach, mine], key_value[head, reach, :HDIM]).astype(BF16)

    def key_grads(head, part):
        cols = slice(head * HDIM, (head + 1) * HDIM)
        here = slice(part * PAIR, (part + 1) * PAIR)
        near = slice(max(0, part - 1) * PAIR, min(2, part + 1) * PAIR)
        g_key = dot(score_t[head, here, near], query[near, cols]).astype(BF16)
        g_value = dot(prob_t[head, here, near], d_mixed[near, cols]).astype(BF16)
        if part == 0:
            border_grads[0, :WIN, cols], border_grads[1, :WIN, cols] = g_key[:WIN], g_value[:WIN]
            grad_key[:WIN, cols], grad_value[:WIN, cols] = g_key[WIN:], g_value[WIN:]
        elif part == 1:
            grad_key[WIN : WIN + PAIR, cols], grad_value[WIN : WIN + PAIR, cols] = g_key, g_value
        else:
            grad_key[ROWS - WIN :, cols], grad_value[ROWS - WIN :, cols] = g_key[:WIN], g_value[:WIN]
            border_grads[0, WIN:, cols], border_grads[1, WIN:, cols] = g_key[WIN:], g_value[WIN:]

    lay_out(0)
    lay_out(1)
    first = [products(0, i) for i in range(blocks)]
    second = []
    for i in range(blocks):
        soften(0, i, first[i])
        second.append(products(1, i))
    jobs = [(query_grads, 0), (query_grads, 1), (key_grads, 0), (key_grads, 1), (key_grads, 2)]
    for i in range(blocks):
        soften(1, i, second[i])
        for job, part in jobs[i : i + 1] if i < 3 else jobs[3:]:
            job(0, part)
    for job, part in jobs:
        job(1, part)
    half = D // 2
    for out, rows in ((sent, slice(half, D)), (kept, slice(0, half))):
        out[0] = dot(ordered[rows], grad_query[...]).astype(BF16)
        out[1] = (dot(ordered[rows], grad_key[...]) + dot(ordered_border[rows], border_grads[0])).astype(BF16)
        out[2] = (dot(ordered[rows], grad_value[...]) + dot(ordered_border[rows], border_grads[1])).astype(BF16)


def attend(length, target, low, high, ordered, query, keys, values, d_mixed, w_key, w_value):
    own = jax.ShapeDtypeStruct((ROWS, D), BF16)
    half = jax.ShapeDtypeStruct((3, D // 2, D), BF16)
    reach = ROWS + 2 * WIN
    return call(
        attend_body,
        [own] * 3 + [jax.ShapeDtypeStruct((2, 2 * WIN, D), BF16)] + [half] * 2,
        (length, target, low, high, ordered, query, keys, values, d_mixed, w_key, w_value),
        [SCALAR, SCALAR, whole(WIN, D), whole(WIN, D), whole(D, ROWS)] + [columns(ROWS)] * 4 + [columns(D)] * 2,
        [columns(ROWS)] * 3
        + [pl.BlockSpec((2, 2 * WIN, PAIR), lambda j: (0, 0, j))]
        + [pl.BlockSpec((3, D // 2, PAIR), lambda j: (0, 0, j))] * 2,
        [
            pltpu.VMEM((D, 2 * WIN), BF16),
            pltpu.VMEM((2 * WIN, D), BF16),
            pltpu.VMEM((2, reach, PAIR), BF16),
            pltpu.VMEM((2, 2 * ROWS, PAIR), BF16),
            pltpu.VMEM((2, reach, ROWS), BF16),
            pltpu.VMEM((2, reach, ROWS), BF16),
        ],
        D * D * (ROWS * 3 + WIN * 8) + 10 * 4 * 3 * HEADS * WIN**3,
        room=ROOM[2],
    )


def back_body(grad_query, grad_key, grad_value, border_grads, w_query, w_key, w_value, total, sides, border_total):
    part = dot_nt(grad_query[...], w_query[...]) + dot_nt(grad_key[...], w_key[...]) + dot_nt(grad_value[...], w_value[...])
    border_part = dot_nt(border_grads[0], w_key[...]) + dot_nt(border_grads[1], w_value[...])

    @pl.when(pl.program_id(0) == 0)
    def _():
        total[...] = part
        border_total[...] = border_part

    @pl.when(pl.program_id(0) > 0)
    def _():
        total[...] += part
        border_total[...] += border_part

    @pl.when(pl.program_id(0) == STEPS - 1)
    def _():
        sides[...] = border_total[...].astype(BF16)


def back(*ins):
    return call(
        back_body,
        [jax.ShapeDtypeStruct((ROWS, D), F32), jax.ShapeDtypeStruct((2 * WIN, D), BF16)],
        ins,
        [columns(ROWS)] * 3 + [pl.BlockSpec((2, 2 * WIN, PAIR), lambda j: (0, 0, j))] + [columns(D)] * 3,
        [whole(ROWS, D), whole(2 * WIN, D)],
        [pltpu.VMEM((2 * WIN, D), F32)],
        (3 * ROWS + 4 * WIN) * D * D,
    )


def finish_body(frames, grads, d_hidden, near, out):
    normed, inverse = normalize(frames[...])
    part = pl.program_id(0)
    inner = jnp.logical_and(part > 0, part < STEPS - 1)
    d_rows = d_hidden[...] + jnp.where(inner, 0.0, near[...].astype(F32))
    mean_grad = jnp.mean(d_rows, -1, keepdims=True)
    mean_cross = jnp.mean(d_rows * normed, -1, keepdims=True)
    out[...] = (grads[...].astype(F32) + inverse * (d_rows - mean_grad - normed * mean_cross)).astype(BF16)


def finish(frames, grads, d_hidden, near):
    block = pl.BlockSpec((WIN, D), lambda j: (j, 0))
    return call(
        finish_body,
        jax.ShapeDtypeStruct((ROWS, D), BF16),
        (frames, grads, d_hidden, near),
        [block] * 3 + [pl.BlockSpec((WIN, D), lambda j: (j // (STEPS - 1), 0))],
        block,
        [],
        ROWS * D * 16,
    )


def swap(first, last, pairs):
    count = lax.axis_size("tm")
    even = lax.axis_index("tm") % 2 == 0
    if pairs == 0:
        return lax.ppermute(jnp.where(even, last, first), "tm", [(i, i ^ 1) for i in range(count)])
    across = [(i, i + 1 if i % 2 else i - 1) for i in range(1, count - 1)]
    return lax.ppermute(jnp.where(even, first, last), "tm", across)


def in_order(within, across):
    even = lax.axis_index("tm") % 2 == 0
    return jnp.where(even, across, within), jnp.where(even, within, across)


def in_hbm(*arrays):
    return [pltpu.with_memory_space_constraint(array, pltpu.HBM) for array in arrays]


def shards(frames, cotangent, lengths, w_query, w_key, w_value, w_out):
    rows, grads = frames[0], cotangent[0]
    w_query, w_key, w_value, w_out = in_hbm(w_query, w_key, w_value, w_out)
    top, end = rows[:WIN], rows[ROWS - WIN :]
    within, across = swap(top, end, 0), swap(top, end, 1)
    target = block_targets()
    ordered, query, keys, values, d_mixed = front(lengths, target, *in_hbm(rows, grads), w_query, w_key, w_value, w_out)
    low, high = in_order(within, across)
    grad_query, grad_key, grad_value, border_grads, kept, sent = attend(
        lengths, target, low, high, ordered, query, keys, values, d_mixed, w_key, w_value
    )
    got = exchange(sent, (CORE, CORE))
    d_hidden, sides = back(grad_query, grad_key, grad_value, border_grads, w_query, w_key, w_value)
    own = add(kept, got)

    def first(after, _):
        return swap(sides[:WIN], sides[WIN:], 0), swap(sides[:WIN], sides[WIN:], 1)

    def second(after, both):
        now, _ = lax.optimization_barrier((both, after))
        return finish(rows, grads, d_hidden, jnp.concatenate(in_order(*now)))

    def third(after, done):
        return done

    weight_part, grad_frames = scatter_sum([own[0], own[1], own[2]], (first, second, third))
    return (grad_frames[None], weight_part)


def solution(mesh):
    placed = (P("rec", "tm", None), P("rec", "tm", None), P("rec"), P(), P(), P(), P())
    return jax.shard_map(
        shards,
        mesh=mesh,
        in_specs=placed,
        out_specs=(P("rec", "tm", None), P(("rec", "tm"), None)),
        check_vma=False,
    )
```

```python
import functools
import math

import jax
import jax.numpy as jnp
from jax import lax
from jax.experimental import pallas as pl
from jax.experimental.pallas import tpu as pltpu
from jax.sharding import PartitionSpec as P

HEADS = 8
WIN = 128
HDIM = 128
ROWS = 512
D = 1024
PAIR = 2 * HDIM
STEPS = HEADS // 2
epsilon = 1e-05
masked_value = -1e30
F32 = jnp.float32
BF16 = jnp.bfloat16
ROOM = (30, 30, 30, 30)

AXES = ("rec", "tm")
CORE = 32
NEAR = ((16, 4, 1), (80, 12, 3))


def order_of(core):
    return NEAR[core] + NEAR[1 - core]


def exchange(value, masks):
    count = lax.axis_size(AXES)
    pairs = [(i, i ^ masks[(i // CORE) % 2]) for i in range(count)]
    return lax.ppermute(value, AXES, pairs)


def coordinates(device, core):
    high = [(device >> bit) & 1 for bit in (6, 3, 1)]
    low = [(device >> bit) & 1 for bit in (4, 2, 0)]
    return high if core == 0 else [a ^ b for a, b in zip(high, low)]


def block_targets():
    me = lax.axis_index(AXES)
    block = jnp.arange(128, dtype=jnp.int32)
    far = block >> 6
    core = ((me >> 5) & 1) ^ far
    target = me ^ (far * CORE)
    for bit in range(6):
        masks = order_of(0)[bit], order_of(1)[bit]
        move = (block >> (5 - bit)) & 1
        if bit >= 3:
            zero, one = coordinates(me, 0)[bit - 3], coordinates(me, 1)[bit - 3]
            move = move ^ (zero + core * (one - zero))
        target = target ^ (move * (masks[0] + core * (masks[1] - masks[0])))
    return target


def last_groups():
    groups = []
    for device in range(128):
        core = (device // CORE) % 2
        if not any(coordinates(device, core)):
            one, two, three = order_of(core)[3:]
            groups.append([device ^ (a * one) ^ (b * two) ^ (c * three) for a in (0, 1) for b in (0, 1) for c in (0, 1)])
    return groups


def halves(value, dim):
    return lax.index_in_dim(value, 0, dim, False), lax.index_in_dim(value, 1, dim, False)


def add(a, b):
    return (a.astype(jnp.float32) + b.astype(jnp.float32)).astype(jnp.bfloat16)


def scatter_sum(parts, beside):
    masks = list(zip(order_of(0), order_of(1)))
    values = [part.reshape(2, 2, 2, 8, 8, -1) for part in parts]
    left = [[0, 1, 2] for _ in values]
    other = None
    for step in range(3):
        sent = []
        for part in range(3):
            bit = (part + step) % 3
            keep, send = halves(values[part], left[part].index(bit))
            left[part].remove(bit)
            sent.append((keep, exchange(send, masks[bit])))
        other, ready = beside[step](values, other)
        arrived = tie([got for _, got in sent], ready)
        values = [add(keep, got) for (keep, _), got in zip(sent, arrived)]
    value = jnp.concatenate(values, -1)
    got = lax.all_to_all(value.reshape(64, -1), AXES, 0, 0, axis_index_groups=last_groups(), tiled=True)
    chosen = jnp.arange(64)[None, :] % 8 == jnp.arange(8)[:, None]
    return jnp.dot(chosen.astype(got.dtype), got, preferred_element_type=jnp.float32), other


def dot(a, b):
    return lax.dot_general(a, b, (((1,), (0,)), ((), ())), preferred_element_type=F32)


def dot_nt(a, b):
    return lax.dot_general(a, b, (((1,), (1,)), ((), ())), preferred_element_type=F32)


def dot_tn(a, b):
    return lax.dot_general(a, b, (((0,), (0,)), ((), ())), preferred_element_type=F32)


def normalize(rows):
    values = rows.astype(F32)
    center = values - jnp.mean(values, -1, keepdims=True)
    inverse = lax.rsqrt(jnp.mean(center * center, -1, keepdims=True) + epsilon)
    return center * inverse, inverse


def call(body, outs, ins, in_specs, out_specs, scratch, macs, steps=STEPS, room=30):
    size = sum(math.prod(x.shape) * x.dtype.itemsize for x in (*ins, *jax.tree.leaves(outs)))
    return pl.pallas_call(
        body,
        out_shape=outs,
        grid=(steps,),
        in_specs=in_specs,
        out_specs=out_specs,
        scratch_shapes=scratch,
        compiler_params=pltpu.CompilerParams(vmem_limit_bytes=room * 2**20),
        cost_estimate=pl.CostEstimate(flops=2 * macs, bytes_accessed=size, transcendentals=0),
    )(*ins)


def whole(*shape):
    return pl.BlockSpec(shape, lambda j: (0,) * len(shape))


def columns(rows):
    return pl.BlockSpec((rows, PAIR), lambda j: (0, j))


SCALAR = pl.BlockSpec(memory_space=pltpu.SMEM)
HELD = pl.BlockSpec(memory_space=pltpu.VMEM)
AFTER = pl.BlockSpec(memory_space=pl.ANY)


def one_hot(target, first, blocks):
    lane = lax.broadcasted_iota(jnp.int32, (8, D), 1) - lax.broadcasted_iota(jnp.int32, (8, D), 0)
    rows = [jnp.where(lane == 8 * target[first + block], 1.0, 0.0) for block in range(blocks)]
    return jnp.concatenate(rows, 0).astype(BF16)


def here():
    return lax.axis_index("tm") * ROWS


def tie_body(*refs):
    pass


def tie(values, after):
    return pl.pallas_call(
        tie_body,
        out_shape=[jax.ShapeDtypeStruct(value.shape, value.dtype) for value in values],
        in_specs=[AFTER] * (len(values) + 1),
        out_specs=[AFTER] * len(values),
        input_output_aliases={i: i for i in range(len(values))},
        compiler_params=pltpu.CompilerParams(vmem_limit_bytes=2**20),
        cost_estimate=pl.CostEstimate(flops=0, bytes_accessed=0, transcendentals=0),
    )(*values, after)


def front_body(length, target, frames, grads, w_query, w_key, w_value, w_out, ordered, query, keys, values, d_mixed, hidden, masked):
    @pl.when(pl.program_id(0) == 0)
    def _():
        hidden[...] = normalize(frames[...])[0].astype(BF16)
        row = lax.broadcasted_iota(jnp.int32, (ROWS, D), 0) + here()
        masked[...] = jnp.where(row < length[0], grads[...].astype(F32), 0.0).astype(BF16)

    rows = hidden[...]
    d_mixed[...] = dot_nt(masked[...], w_out[...]).astype(BF16)
    query[...] = dot(rows, w_query[...]).astype(BF16)
    keys[...] = dot(rows, w_key[...]).astype(BF16)
    values[...] = dot(rows, w_value[...]).astype(BF16)
    ordered[...] = dot_nt(one_hot(target, pl.program_id(0) * (PAIR // 8), PAIR // 8), rows).astype(BF16)


def front(length, target, frames, grads, w_query, w_key, w_value, w_out):
    wide = jax.ShapeDtypeStruct((ROWS, D), BF16)
    return call(
        front_body,
        [jax.ShapeDtypeStruct((D, ROWS), BF16), wide, wide, wide, wide],
        (length, target, frames, grads, w_query, w_key, w_value, w_out),
        [SCALAR, SCALAR, whole(ROWS, D), whole(ROWS, D)] + [columns(D)] * 3 + [pl.BlockSpec((PAIR, D), lambda j: (j, 0))],
        [pl.BlockSpec((PAIR, ROWS), lambda j: (j, 0))] + [columns(ROWS)] * 4,
        [pltpu.VMEM((ROWS, D), BF16)] * 2,
        5 * ROWS * D * D,
        room=ROOM[0],
    )


def attend_body(
    length, target, low, high, query, keys, values, d_mixed, w_key, w_value,
    grad_query, grad_key, grad_value, border_grads, ordered_border,
    hidden_border, key_value, pair, score_t, prob_t,
):
    scale = HDIM ** (-0.5)
    blocks = ROWS // WIN

    @pl.when(pl.program_id(0) == 0)
    def _():
        hidden_border[:WIN] = normalize(low[...])[0].astype(BF16)
        hidden_border[WIN:] = normalize(high[...])[0].astype(BF16)
        for part in range(4):
            rows = slice(part * PAIR, (part + 1) * PAIR)
            ordered_border[rows] = dot_nt(one_hot(target, part * (PAIR // 8), PAIR // 8), hidden_border[...]).astype(BF16)
        for ref in (pair, score_t, prob_t):
            ref[...] = jnp.zeros_like(ref)

    key_border = dot(hidden_border[...], w_key[...]).astype(BF16)
    value_border = dot(hidden_border[...], w_value[...]).astype(BF16)
    above = lax.broadcasted_iota(jnp.int32, (3 * WIN, WIN), 0)
    lane = lax.broadcasted_iota(jnp.int32, (1, WIN), 1)

    def lay_out(head):
        cols = slice(head * HDIM, (head + 1) * HDIM)
        for side, own, to in ((key_border, keys, slice(0, HDIM)), (value_border, values, slice(HDIM, PAIR))):
            key_value[head, :WIN, to] = side[:WIN, cols]
            key_value[head, WIN : WIN + ROWS, to] = own[:, cols]
            key_value[head, WIN + ROWS :, to] = side[WIN:, cols]
        for i in range(blocks):
            mine = slice(i * WIN, (i + 1) * WIN)
            pair[head, i * PAIR : i * PAIR + WIN, :HDIM] = query[mine, cols]
            pair[head, i * PAIR + WIN : (i + 1) * PAIR, HDIM:] = d_mixed[mine, cols]

    def products(head, i):
        return dot_nt(key_value[head, i * WIN : (i + 3) * WIN], pair[head, i * PAIR : (i + 1) * PAIR])

    def soften(head, i, both):
        mine = slice(i * WIN, (i + 1) * WIN)
        reach = slice(i * WIN, (i + 3) * WIN)
        first = (1 - i) * WIN - here()
        last = length[0] - here() + (1 - i) * WIN - 1
        allowed = (above >= jnp.maximum(lane, first)) & (above <= jnp.minimum(lane + 2 * WIN, last))
        scores = jnp.where(allowed, both[:, :WIN], masked_value)
        d_prob = both[:, WIN:]
        row_max = jnp.max(scores, 0, keepdims=True)
        expo = jnp.exp2((scores - row_max) * (scale * math.log2(math.e)))
        inverse_sum = 1.0 / jnp.sum(expo, 0, keepdims=True)
        row_delta = jnp.sum(expo * d_prob, 0, keepdims=True) * inverse_sum
        score_t[head, reach, mine] = (expo * (inverse_sum * scale) * (d_prob - row_delta)).astype(BF16)
        prob_t[head, reach, mine] = (expo * inverse_sum).astype(BF16)

    def query_grads(head, part):
        cols = slice(head * HDIM, (head + 1) * HDIM)
        mine = slice(part * PAIR, (part + 1) * PAIR)
        reach = slice(part * PAIR, part * PAIR + 2 * PAIR)
        grad_query[mine, cols] = dot_tn(score_t[head, reach, mine], key_value[head, reach, :HDIM]).astype(BF16)

    def key_grads(head, part):
        cols = slice(head * HDIM, (head + 1) * HDIM)
        here = slice(part * PAIR, (part + 1) * PAIR)
        near = slice(max(0, part - 1) * PAIR, min(2, part + 1) * PAIR)
        g_key = dot(score_t[head, here, near], query[near, cols]).astype(BF16)
        g_value = dot(prob_t[head, here, near], d_mixed[near, cols]).astype(BF16)
        if part == 0:
            border_grads[0, :WIN, cols], border_grads[1, :WIN, cols] = g_key[:WIN], g_value[:WIN]
            grad_key[:WIN, cols], grad_value[:WIN, cols] = g_key[WIN:], g_value[WIN:]
        elif part == 1:
            grad_key[WIN : WIN + PAIR, cols], grad_value[WIN : WIN + PAIR, cols] = g_key, g_value
        else:
            grad_key[ROWS - WIN :, cols], grad_value[ROWS - WIN :, cols] = g_key[:WIN], g_value[:WIN]
            border_grads[0, WIN:, cols], border_grads[1, WIN:, cols] = g_key[WIN:], g_value[WIN:]

    lay_out(0)
    lay_out(1)
    first = [products(0, i) for i in range(blocks)]
    second = []
    for i in range(blocks):
        soften(0, i, first[i])
        second.append(products(1, i))
    jobs = [(query_grads, 0), (query_grads, 1), (key_grads, 0), (key_grads, 1), (key_grads, 2)]
    for i in range(blocks):
        soften(1, i, second[i])
        for job, part in jobs[i : i + 1] if i < 3 else jobs[3:]:
            job(0, part)
    for job, part in jobs:
        job(1, part)


def attend(length, target, low, high, query, keys, values, d_mixed, w_key, w_value):
    own = jax.ShapeDtypeStruct((ROWS, D), BF16)
    reach = ROWS + 2 * WIN
    return call(
        attend_body,
        [own] * 3 + [jax.ShapeDtypeStruct((2, 2 * WIN, D), BF16), jax.ShapeDtypeStruct((D, 2 * WIN), BF16)],
        (length, target, low, high, query, keys, values, d_mixed, w_key, w_value),
        [SCALAR, SCALAR, whole(WIN, D), whole(WIN, D)] + [columns(ROWS)] * 4 + [columns(D)] * 2,
        [columns(ROWS)] * 3 + [pl.BlockSpec((2, 2 * WIN, PAIR), lambda j: (0, 0, j)), whole(D, 2 * WIN)],
        [
            pltpu.VMEM((2 * WIN, D), BF16),
            pltpu.VMEM((2, reach, PAIR), BF16),
            pltpu.VMEM((2, 2 * ROWS, PAIR), BF16),
            pltpu.VMEM((2, reach, ROWS), BF16),
            pltpu.VMEM((2, reach, ROWS), BF16),
        ],
        D * D * WIN * 4 + 10 * 4 * 3 * HEADS * WIN**3,
        room=ROOM[2],
    )


def pair_columns():
    return pl.ds(pl.multiple_of(pl.program_id(0) * PAIR, PAIR), PAIR)


def project_body(ordered, grad, kept, sent):
    half = D // 2
    columns = grad[:, pair_columns()]
    sent[...] = dot(ordered[half:], columns).astype(BF16)
    kept[...] = dot(ordered[:half], columns).astype(BF16)


def project_border_body(part, ordered, grad, ordered_border, border_grads, kept, sent):
    half = D // 2
    columns, border_columns = grad[:, pair_columns()], border_grads[part, :, pair_columns()]
    for out, rows in ((sent, slice(half, D)), (kept, slice(0, half))):
        out[...] = (dot(ordered[rows], columns) + dot(ordered_border[rows], border_columns)).astype(BF16)


def project(ordered, grad, ordered_border=None, border_grads=None, part=0):
    half = jax.ShapeDtypeStruct((D // 2, D), BF16)
    if ordered_border is None:
        body, ins = project_body, (ordered, grad)
    else:
        body, ins = functools.partial(project_border_body, part), (ordered, grad, ordered_border, border_grads)
    return call(body, [half] * 2, ins, [HELD] * len(ins), [columns(D // 2)] * 2, [], D * D * (ROWS + 2 * WIN), room=20)


def back_body(grad_query, grad_key, grad_value, w_query, w_key, w_value, *rest):
    total = rest[-1]
    total[...] = (
        dot_nt(grad_query[...], w_query[...]) + dot_nt(grad_key[...], w_key[...]) + dot_nt(grad_value[...], w_value[...])
    )


def rows_of(columns):
    return pl.BlockSpec((PAIR, columns), lambda j: (j, 0))


def back(*ins):
    return call(
        back_body,
        jax.ShapeDtypeStruct((ROWS, D), F32),
        ins,
        [HELD] * 3 + [rows_of(D)] * 3 + [AFTER] * 3,
        columns(ROWS),
        [],
        3 * ROWS * D * D,
        room=24,
    )


def back_border_body(grads, w_key, w_value, *rest):
    sides = rest[-1]
    sides[...] = (dot_nt(grads[0], w_key[...]) + dot_nt(grads[1], w_value[...])).astype(BF16)


def back_border(*ins):
    return call(
        back_border_body,
        jax.ShapeDtypeStruct((2 * WIN, D), BF16),
        ins,
        [HELD] + [rows_of(D)] * 2 + [AFTER] * 3,
        columns(2 * WIN),
        [],
        4 * WIN * D * D,
        room=16,
    )


def finish_body(frames, grads, d_hidden, near, after, out):
    normed, inverse = normalize(frames[...])
    part = pl.program_id(0)
    inner = jnp.logical_and(part > 0, part < STEPS - 1)
    d_rows = d_hidden[...] + jnp.where(inner, 0.0, near[...].astype(F32))
    mean_grad = jnp.mean(d_rows, -1, keepdims=True)
    mean_cross = jnp.mean(d_rows * normed, -1, keepdims=True)
    out[...] = (grads[...].astype(F32) + inverse * (d_rows - mean_grad - normed * mean_cross)).astype(BF16)


def finish(frames, grads, d_hidden, near, after):
    block = pl.BlockSpec((WIN, D), lambda j: (j, 0))
    return call(
        finish_body,
        jax.ShapeDtypeStruct((ROWS, D), BF16),
        (frames, grads, d_hidden, near, after),
        [block] * 3 + [pl.BlockSpec((WIN, D), lambda j: (j // (STEPS - 1), 0)), AFTER],
        block,
        [],
        ROWS * D * 16,
        room=16,
    )


def swap(first, last, pairs):
    even = lax.axis_index("tm") % 2 == 0
    return send(jnp.where(even, last, first) if pairs == 0 else jnp.where(even, first, last), pairs)


def send(rows, pairs):
    count = lax.axis_size("tm")
    if pairs == 0:
        return lax.ppermute(rows, "tm", [(i, i ^ 1) for i in range(count)])
    return lax.ppermute(rows, "tm", [(i, i + 1 if i % 2 else i - 1) for i in range(1, count - 1)])


def choose_body(sides, *rest):
    within, across = rest[-2:]
    even = lax.axis_index("tm") % 2 == 0

    @pl.when(even)
    def _():
        within[...] = sides[WIN:]
        across[...] = sides[:WIN]

    @pl.when(jnp.logical_not(even))
    def _():
        within[...] = sides[:WIN]
        across[...] = sides[WIN:]


def choose(sides, *after):
    half = jax.ShapeDtypeStruct((WIN, D), BF16)
    return call(choose_body, [half] * 2, (sides, *after), [whole(2 * WIN, D)] + [AFTER] * 3, [whole(WIN, D)] * 2, [], 0, steps=1, room=8)


def in_order(within, across):
    even = lax.axis_index("tm") % 2 == 0
    return jnp.where(even, across, within), jnp.where(even, within, across)


def in_hbm(*arrays):
    return [pltpu.with_memory_space_constraint(array, pltpu.HBM) for array in arrays]


def shards(frames, cotangent, lengths, w_query, w_key, w_value, w_out):
    rows, grads = frames[0], cotangent[0]
    w_query, w_key, w_value, w_out = in_hbm(w_query, w_key, w_value, w_out)
    top, end = rows[:WIN], rows[ROWS - WIN :]
    within, across = swap(top, end, 0), swap(top, end, 1)
    target = block_targets()
    ordered, query, keys, values, d_mixed = front(lengths, target, *in_hbm(rows, grads), w_query, w_key, w_value, w_out)
    low, high = in_order(within, across)
    grad_query, grad_key, grad_value, border_grads, ordered_border = attend(
        lengths, target, low, high, query, keys, values, d_mixed, w_key, w_value
    )
    shares = [
        project(ordered, grad_query),
        project(ordered, grad_key, ordered_border, border_grads, 0),
        project(ordered, grad_value, ordered_border, border_grads, 1),
    ]
    own = [add(kept, exchange(sent, (CORE, CORE))) for kept, sent in shares]

    def first(after, _):
        d_hidden = back(grad_query, grad_key, grad_value, w_query, w_key, w_value, *after)
        return d_hidden, d_hidden

    def second(after, d_hidden):
        sides = back_border(border_grads, w_key, w_value, *after)
        return (d_hidden, sides), sides

    def third(after, before):
        d_hidden, sides = before
        within, across = choose(sides, *after)
        return (d_hidden, send(within, 0), send(across, 1)), within

    weight_part, (d_hidden, within, across) = scatter_sum(own, (first, second, third))
    grad_frames = finish(rows, grads, d_hidden, jnp.concatenate(in_order(within, across)), own[2])
    return (grad_frames[None], weight_part)


def solution(mesh):
    placed = (P("rec", "tm", None), P("rec", "tm", None), P("rec"), P(), P(), P(), P())
    return jax.shard_map(
        shards,
        mesh=mesh,
        in_specs=placed,
        out_specs=(P("rec", "tm", None), P(("rec", "tm"), None)),
        check_vma=False,
    )
```

```python
import functools
import math

import jax
import jax.numpy as jnp
from jax import lax
from jax.experimental import pallas as pl
from jax.experimental.pallas import tpu as pltpu
from jax.sharding import PartitionSpec as P

HEADS = 8
WIN = 128
HDIM = 128
ROWS = 512
D = 1024
PAIR = 2 * HDIM
STEPS = HEADS // 2
epsilon = 1e-05
masked_value = -1e30
F32 = jnp.float32
BF16 = jnp.bfloat16
ROOM = (30, 30, 30, 30)

AXES = ("rec", "tm")
CORE = 32
NEAR = ((16, 4, 1), (80, 12, 3))


def order_of(core):
    return NEAR[core] + NEAR[1 - core]


def exchange(value, masks):
    count = lax.axis_size(AXES)
    pairs = [(i, i ^ masks[(i // CORE) % 2]) for i in range(count)]
    return lax.ppermute(value, AXES, pairs)


def coordinates(device, core):
    high = [(device >> bit) & 1 for bit in (6, 3, 1)]
    low = [(device >> bit) & 1 for bit in (4, 2, 0)]
    return high if core == 0 else [a ^ b for a, b in zip(high, low)]


def block_targets():
    me = lax.axis_index(AXES)
    block = jnp.arange(128, dtype=jnp.int32)
    far = block >> 6
    core = ((me >> 5) & 1) ^ far
    target = me ^ (far * CORE)
    for bit in range(6):
        masks = order_of(0)[bit], order_of(1)[bit]
        move = (block >> (5 - bit)) & 1
        if bit >= 3:
            zero, one = coordinates(me, 0)[bit - 3], coordinates(me, 1)[bit - 3]
            move = move ^ (zero + core * (one - zero))
        target = target ^ (move * (masks[0] + core * (masks[1] - masks[0])))
    return target


def last_groups():
    groups = []
    for device in range(128):
        core = (device // CORE) % 2
        if not any(coordinates(device, core)):
            one, two, three = order_of(core)[3:]
            groups.append([device ^ (a * one) ^ (b * two) ^ (c * three) for a in (0, 1) for b in (0, 1) for c in (0, 1)])
    return groups


def total(terms):
    return sum((term.astype(jnp.float32) for term in terms[1:]), terms[0].astype(jnp.float32)).astype(jnp.bfloat16)


def split(terms, dim):
    shape = [term.reshape(2, 2, 2, 8, 8, -1) if term.ndim == 2 else term for term in terms]
    stay = [lax.index_in_dim(term, 0, dim, False) for term in shape]
    return stay, total([lax.index_in_dim(term, 1, dim, False) for term in shape])


def scatter_sum(first, beside):
    masks = list(zip(order_of(0), order_of(1)))
    left = [[bit for bit in range(3) if bit != part] for part in range(3)]
    parts, other = first, None
    for step in range(3):
        got = [exchange(go, masks[(part + step) % 3]) for part, (_, go) in enumerate(parts)]
        other, ready = beside[step]([go for _, go in parts], other)
        values = [stay + [come] for (stay, _), come in zip(parts, tie(got, ready))]
        if step < 2:
            parts = []
            for part, terms in enumerate(values):
                bit = (part + step + 1) % 3
                parts.append(split(terms, left[part].index(bit)))
                left[part].remove(bit)
    values = [total(terms) for terms in values]
    value = jnp.concatenate(values, -1)
    got = lax.all_to_all(value.reshape(64, -1), AXES, 0, 0, axis_index_groups=last_groups(), tiled=True)
    chosen = jnp.arange(64)[None, :] % 8 == jnp.arange(8)[:, None]
    return jnp.dot(chosen.astype(got.dtype), got, preferred_element_type=jnp.float32), other


def dot(a, b):
    return lax.dot_general(a, b, (((1,), (0,)), ((), ())), preferred_element_type=F32)


def dot_nt(a, b):
    return lax.dot_general(a, b, (((1,), (1,)), ((), ())), preferred_element_type=F32)


def dot_tn(a, b):
    return lax.dot_general(a, b, (((0,), (0,)), ((), ())), preferred_element_type=F32)


def normalize(rows):
    values = rows.astype(F32)
    center = values - jnp.mean(values, -1, keepdims=True)
    inverse = lax.rsqrt(jnp.mean(center * center, -1, keepdims=True) + epsilon)
    return center * inverse, inverse


def call(body, outs, ins, in_specs, out_specs, scratch, macs, steps=STEPS, room=30):
    size = sum(math.prod(x.shape) * x.dtype.itemsize for x in (*ins, *jax.tree.leaves(outs)))
    return pl.pallas_call(
        body,
        out_shape=outs,
        grid=(steps,),
        in_specs=in_specs,
        out_specs=out_specs,
        scratch_shapes=scratch,
        compiler_params=pltpu.CompilerParams(vmem_limit_bytes=room * 2**20),
        cost_estimate=pl.CostEstimate(flops=2 * macs, bytes_accessed=size, transcendentals=0),
    )(*ins)


def whole(*shape):
    return pl.BlockSpec(shape, lambda j: (0,) * len(shape))


def columns(rows):
    return pl.BlockSpec((rows, PAIR), lambda j: (0, j))


SCALAR = pl.BlockSpec(memory_space=pltpu.SMEM)
HELD = pl.BlockSpec(memory_space=pltpu.VMEM)
AFTER = pl.BlockSpec(memory_space=pl.ANY)


def one_hot(target, first, blocks):
    lane = lax.broadcasted_iota(jnp.int32, (8, D), 1) - lax.broadcasted_iota(jnp.int32, (8, D), 0)
    rows = [jnp.where(lane == 8 * target[first + block], 1.0, 0.0) for block in range(blocks)]
    return jnp.concatenate(rows, 0).astype(BF16)


def here():
    return lax.axis_index("tm") * ROWS


def tie_body(*refs):
    pass


def tie(values, after):
    return pl.pallas_call(
        tie_body,
        out_shape=[jax.ShapeDtypeStruct(value.shape, value.dtype) for value in values],
        in_specs=[AFTER] * (len(values) + 1),
        out_specs=[AFTER] * len(values),
        input_output_aliases={i: i for i in range(len(values))},
        compiler_params=pltpu.CompilerParams(vmem_limit_bytes=2**20),
        cost_estimate=pl.CostEstimate(flops=0, bytes_accessed=0, transcendentals=0),
    )(*values, after)


def front_body(length, target, frames, grads, w_query, w_key, w_value, w_out, ordered, query, keys, values, d_mixed, hidden, masked):
    @pl.when(pl.program_id(0) == 0)
    def _():
        hidden[...] = normalize(frames[...])[0].astype(BF16)
        row = lax.broadcasted_iota(jnp.int32, (ROWS, D), 0) + here()
        masked[...] = jnp.where(row < length[0], grads[...].astype(F32), 0.0).astype(BF16)

    rows = hidden[...]
    d_mixed[...] = dot_nt(masked[...], w_out[...]).astype(BF16)
    query[...] = dot(rows, w_query[...]).astype(BF16)
    keys[...] = dot(rows, w_key[...]).astype(BF16)
    values[...] = dot(rows, w_value[...]).astype(BF16)
    ordered[...] = dot_nt(one_hot(target, pl.program_id(0) * (PAIR // 8), PAIR // 8), rows).astype(BF16)


def front(length, target, frames, grads, w_query, w_key, w_value, w_out):
    wide = jax.ShapeDtypeStruct((ROWS, D), BF16)
    return call(
        front_body,
        [jax.ShapeDtypeStruct((D, ROWS), BF16), wide, wide, wide, wide],
        (length, target, frames, grads, w_query, w_key, w_value, w_out),
        [SCALAR, SCALAR, whole(ROWS, D), whole(ROWS, D)] + [columns(D)] * 3 + [pl.BlockSpec((PAIR, D), lambda j: (j, 0))],
        [pl.BlockSpec((PAIR, ROWS), lambda j: (j, 0))] + [columns(ROWS)] * 4,
        [pltpu.VMEM((ROWS, D), BF16)] * 2,
        5 * ROWS * D * D,
        room=ROOM[0],
    )


def pair_columns():
    return pl.ds(pl.multiple_of(pl.program_id(0) * PAIR, PAIR), PAIR)


def attend_body(
    length, target, low, high, query_all, keys_all, values_all, d_mixed_all, w_key, w_value,
    grad_query, grad_key, grad_value, border_grads, ordered_border,
    hidden_border, key_value, pair, score_t, prob_t,
):
    scale = HDIM ** (-0.5)
    blocks = ROWS // WIN

    @pl.when(pl.program_id(0) == 0)
    def _():
        hidden_border[:WIN] = normalize(low[...])[0].astype(BF16)
        hidden_border[WIN:] = normalize(high[...])[0].astype(BF16)
        for part in range(4):
            rows = slice(part * PAIR, (part + 1) * PAIR)
            ordered_border[rows] = dot_nt(one_hot(target, part * (PAIR // 8), PAIR // 8), hidden_border[...]).astype(BF16)
        pair[...] = jnp.zeros_like(pair)
        outside = jnp.zeros((WIN, WIN), BF16)
        for ref in (score_t, prob_t):
            for head in range(2):
                for i in range(0, blocks, 2):
                    ref[head, (i + 3) * WIN : (i + 4) * WIN, i * WIN : (i + 1) * WIN] = outside
                    ref[head, i * WIN : (i + 1) * WIN, (i + 1) * WIN : (i + 2) * WIN] = outside

    query, keys, values, d_mixed = (
        ref.at[:, pair_columns()] for ref in (query_all, keys_all, values_all, d_mixed_all)
    )
    key_border = dot(hidden_border[...], w_key[...]).astype(BF16)
    value_border = dot(hidden_border[...], w_value[...]).astype(BF16)
    above = lax.broadcasted_iota(jnp.int32, (3 * WIN, WIN), 0)
    lane = lax.broadcasted_iota(jnp.int32, (1, WIN), 1)

    def lay_out(head):
        cols = slice(head * HDIM, (head + 1) * HDIM)
        for side, own, to in ((key_border, keys, slice(0, HDIM)), (value_border, values, slice(HDIM, PAIR))):
            key_value[head, :WIN, to] = side[:WIN, cols]
            key_value[head, WIN : WIN + ROWS, to] = own[:, cols]
            key_value[head, WIN + ROWS :, to] = side[WIN:, cols]
        for i in range(blocks):
            mine = slice(i * WIN, (i + 1) * WIN)
            pair[head, i * PAIR : i * PAIR + WIN, :HDIM] = query[mine, cols]
            pair[head, i * PAIR + WIN : (i + 1) * PAIR, HDIM:] = d_mixed[mine, cols]

    def products(head, i):
        return dot_nt(key_value[head, i * WIN : (i + 3) * WIN], pair[head, i * PAIR : (i + 1) * PAIR])

    def soften(head, i, both):
        mine = slice(i * WIN, (i + 1) * WIN)
        reach = slice(i * WIN, (i + 3) * WIN)
        first = (1 - i) * WIN - here()
        last = length[0] - here() + (1 - i) * WIN - 1
        allowed = (above >= jnp.maximum(lane, first)) & (above <= jnp.minimum(lane + 2 * WIN, last))
        scores = jnp.where(allowed, both[:, :WIN], masked_value)
        d_prob = both[:, WIN:]
        row_max = jnp.max(scores, 0, keepdims=True)
        expo = jnp.exp2((scores - row_max) * (scale * math.log2(math.e)))
        inverse_sum = 1.0 / jnp.sum(expo, 0, keepdims=True)
        row_delta = jnp.sum(expo * d_prob, 0, keepdims=True) * inverse_sum
        score_t[head, reach, mine] = (expo * (inverse_sum * scale) * (d_prob - row_delta)).astype(BF16)
        prob_t[head, reach, mine] = (expo * inverse_sum).astype(BF16)

    def query_grads(head, part):
        cols = slice(head * HDIM, (head + 1) * HDIM)
        mine = slice(part * PAIR, (part + 1) * PAIR)
        reach = slice(part * PAIR, part * PAIR + 2 * PAIR)
        grad_query[mine, cols] = dot_tn(score_t[head, reach, mine], key_value[head, reach, :HDIM]).astype(BF16)

    def key_grads(head, part):
        cols = slice(head * HDIM, (head + 1) * HDIM)
        here = slice(part * PAIR, (part + 1) * PAIR)
        near = slice(max(0, part - 1) * PAIR, min(2, part + 1) * PAIR)
        g_key = dot(score_t[head, here, near], query[near, cols]).astype(BF16)
        g_value = dot(prob_t[head, here, near], d_mixed[near, cols]).astype(BF16)
        if part == 0:
            border_grads[0, :WIN, cols], border_grads[1, :WIN, cols] = g_key[:WIN], g_value[:WIN]
            grad_key[:WIN, cols], grad_value[:WIN, cols] = g_key[WIN:], g_value[WIN:]
        elif part == 1:
            grad_key[WIN : WIN + PAIR, cols], grad_value[WIN : WIN + PAIR, cols] = g_key, g_value
        else:
            grad_key[ROWS - WIN :, cols], grad_value[ROWS - WIN :, cols] = g_key[:WIN], g_value[:WIN]
            border_grads[0, WIN:, cols], border_grads[1, WIN:, cols] = g_key[WIN:], g_value[WIN:]

    lay_out(0)
    lay_out(1)
    first = [products(0, i) for i in range(blocks)]
    second = []
    for i in range(blocks):
        soften(0, i, first[i])
        second.append(products(1, i))
    jobs = [(query_grads, 0), (query_grads, 1), (key_grads, 0), (key_grads, 1), (key_grads, 2)]
    for i in range(blocks):
        soften(1, i, second[i])
        for job, part in jobs[i : i + 1] if i < 3 else jobs[3:]:
            job(0, part)
    for job, part in jobs:
        job(1, part)


def attend(length, target, low, high, query, keys, values, d_mixed, w_key, w_value):
    own = jax.ShapeDtypeStruct((ROWS, D), BF16)
    reach = ROWS + 2 * WIN
    return call(
        attend_body,
        [own] * 3 + [jax.ShapeDtypeStruct((2, 2 * WIN, D), BF16), jax.ShapeDtypeStruct((D, 2 * WIN), BF16)],
        (length, target, low, high, query, keys, values, d_mixed, w_key, w_value),
        [SCALAR, SCALAR, whole(WIN, D), whole(WIN, D)] + [HELD] * 4 + [columns(D)] * 2,
        [columns(ROWS)] * 3 + [pl.BlockSpec((2, 2 * WIN, PAIR), lambda j: (0, 0, j)), whole(D, 2 * WIN)],
        [
            pltpu.VMEM((2 * WIN, D), BF16),
            pltpu.VMEM((2, reach, PAIR), BF16),
            pltpu.VMEM((2, 2 * ROWS, PAIR), BF16),
            pltpu.VMEM((2, reach, ROWS), BF16),
            pltpu.VMEM((2, reach, ROWS), BF16),
        ],
        D * D * WIN * 4 + 10 * 4 * 3 * HEADS * WIN**3,
        room=ROOM[2],
    )


def project_body(ordered, grad, kept, sent):
    half = D // 2
    columns = grad[:, pair_columns()]
    sent[...] = dot(ordered[half:], columns).astype(BF16)
    kept[...] = dot(ordered[:half], columns).astype(BF16)


def project_border_body(part, ordered, grad, ordered_border, border_grads, *rest):
    kept, sent = rest[-2:]
    half = D // 2
    columns, border_columns = grad[:, pair_columns()], border_grads[part - 1, :, pair_columns()]
    for out, rows in ((sent, slice(half, D)), (kept, slice(0, half))):
        out[...] = (dot(ordered[rows], columns) + dot(ordered_border[rows], border_columns)).astype(BF16)


def project(part, *ins):
    half = jax.ShapeDtypeStruct((D // 2, D), BF16)
    body = functools.partial(project_border_body, part) if part else project_body
    specs = [HELD] * min(len(ins), 4) + [AFTER] * (len(ins) - 4)
    return call(body, [half] * 2, ins, specs, [columns(D // 2)] * 2, [], D * D * (ROWS + 2 * WIN), room=20)


def back_body(grad_query, grad_key, grad_value, w_query, w_key, w_value, *rest):
    total = rest[-1]
    total[...] = (
        dot_nt(grad_query[...], w_query[...]) + dot_nt(grad_key[...], w_key[...]) + dot_nt(grad_value[...], w_value[...])
    )


def rows_of(columns):
    return pl.BlockSpec((PAIR, columns), lambda j: (j, 0))


def back(*ins):
    return call(
        back_body,
        jax.ShapeDtypeStruct((ROWS, D), F32),
        ins,
        [HELD] * 3 + [rows_of(D)] * 3 + [AFTER] * 3,
        columns(ROWS),
        [],
        3 * ROWS * D * D,
        room=24,
    )


def back_border_body(grads, w_key, w_value, *rest):
    sides = rest[-1]
    sides[...] = (dot_nt(grads[0], w_key[...]) + dot_nt(grads[1], w_value[...])).astype(BF16)


def back_border(*ins):
    return call(
        back_border_body,
        jax.ShapeDtypeStruct((2 * WIN, D), BF16),
        ins,
        [HELD] + [rows_of(D)] * 2 + [AFTER] * 3,
        columns(2 * WIN),
        [],
        4 * WIN * D * D,
        room=16,
    )


def finish_body(frames, grads, d_hidden, near, after, out):
    normed, inverse = normalize(frames[...])
    part = pl.program_id(0)
    inner = jnp.logical_and(part > 0, part < STEPS - 1)
    d_rows = d_hidden[...] + jnp.where(inner, 0.0, near[...].astype(F32))
    mean_grad = jnp.mean(d_rows, -1, keepdims=True)
    mean_cross = jnp.mean(d_rows * normed, -1, keepdims=True)
    out[...] = (grads[...].astype(F32) + inverse * (d_rows - mean_grad - normed * mean_cross)).astype(BF16)


def finish(frames, grads, d_hidden, near, after):
    block = pl.BlockSpec((WIN, D), lambda j: (j, 0))
    return call(
        finish_body,
        jax.ShapeDtypeStruct((ROWS, D), BF16),
        (frames, grads, d_hidden, near, after),
        [block] * 3 + [pl.BlockSpec((WIN, D), lambda j: (j // (STEPS - 1), 0)), AFTER],
        block,
        [],
        ROWS * D * 16,
        room=16,
    )


def swap(first, last, pairs):
    even = lax.axis_index("tm") % 2 == 0
    return send(jnp.where(even, last, first) if pairs == 0 else jnp.where(even, first, last), pairs)


def send(rows, pairs):
    count = lax.axis_size("tm")
    if pairs == 0:
        return lax.ppermute(rows, "tm", [(i, i ^ 1) for i in range(count)])
    return lax.ppermute(rows, "tm", [(i, i + 1 if i % 2 else i - 1) for i in range(1, count - 1)])


def choose_body(sides, *rest):
    within, across = rest[-2:]
    even = lax.axis_index("tm") % 2 == 0

    @pl.when(even)
    def _():
        within[...] = sides[WIN:]
        across[...] = sides[:WIN]

    @pl.when(jnp.logical_not(even))
    def _():
        within[...] = sides[:WIN]
        across[...] = sides[WIN:]


def choose(sides, *after):
    half = jax.ShapeDtypeStruct((WIN, D), BF16)
    return call(choose_body, [half] * 2, (sides, *after), [whole(2 * WIN, D)] + [AFTER] * 3, [whole(WIN, D)] * 2, [], 0, steps=1, room=8)


def in_order(within, across):
    even = lax.axis_index("tm") % 2 == 0
    return jnp.where(even, across, within), jnp.where(even, within, across)


def in_hbm(*arrays):
    return [pltpu.with_memory_space_constraint(array, pltpu.HBM) for array in arrays]


def shards(frames, cotangent, lengths, w_query, w_key, w_value, w_out):
    rows, grads = frames[0], cotangent[0]
    w_query, w_key, w_value, w_out = in_hbm(w_query, w_key, w_value, w_out)
    top, end = rows[:WIN], rows[ROWS - WIN :]
    within, across = swap(top, end, 0), swap(top, end, 1)
    target = block_targets()
    ordered, query, keys, values, d_mixed = front(lengths, target, *in_hbm(rows, grads), w_query, w_key, w_value, w_out)
    low, high = in_order(within, across)
    grad_query, grad_key, grad_value, border_grads, ordered_border = attend(
        lengths, target, low, high, query, keys, values, d_mixed, w_key, w_value
    )
    parts = []
    for part, ins in enumerate(
        (
            (ordered, grad_query),
            (ordered, grad_key, ordered_border, border_grads),
            (ordered, grad_value, ordered_border, border_grads),
        )
    ):
        kept, sent = project(part, *ins, *(parts[0][1:] if part == 2 else ()))
        parts.append(split([kept, exchange(sent, (CORE, CORE))], part))

    def first(after, _):
        d_hidden = back(grad_query, grad_key, grad_value, w_query, w_key, w_value, *after)
        return d_hidden, d_hidden

    def second(after, d_hidden):
        sides = back_border(border_grads, w_key, w_value, *after)
        return (d_hidden, sides), sides

    def third(after, before):
        d_hidden, sides = before
        within, across = choose(sides, *after)
        return (d_hidden, send(within, 0), send(across, 1)), within

    weight_part, (d_hidden, within, across) = scatter_sum(parts, (first, second, third))
    grad_frames = finish(rows, grads, d_hidden, jnp.concatenate(in_order(within, across)), parts[2][1])
    return (grad_frames[None], weight_part)


def solution(mesh):
    placed = (P("rec", "tm", None), P("rec", "tm", None), P("rec"), P(), P(), P(), P())
    return jax.shard_map(
        shards,
        mesh=mesh,
        in_specs=placed,
        out_specs=(P("rec", "tm", None), P(("rec", "tm"), None)),
        check_vma=False,
    )
```

```python
import functools
import math

import jax
import jax.numpy as jnp
from jax import lax
from jax.experimental import pallas as pl
from jax.experimental.pallas import tpu as pltpu
from jax.sharding import PartitionSpec as P

HEADS = 8
WIN = 128
HDIM = 128
ROWS = 512
D = 1024
PAIR = 2 * HDIM
STEPS = HEADS // 2
epsilon = 1e-05
masked_value = -1e30
F32 = jnp.float32
BF16 = jnp.bfloat16
ROOM = (30, 30, 30, 30)

AXES = ("rec", "tm")
CORE = 32
NEAR = ((16, 4, 1), (80, 12, 3))


def order_of(core):
    return NEAR[core] + NEAR[1 - core]


def exchange(value, masks):
    count = lax.axis_size(AXES)
    pairs = [(i, i ^ masks[(i // CORE) % 2]) for i in range(count)]
    return lax.ppermute(value, AXES, pairs)


def coordinates(device, core):
    high = [(device >> bit) & 1 for bit in (6, 3, 1)]
    low = [(device >> bit) & 1 for bit in (4, 2, 0)]
    return high if core == 0 else [a ^ b for a, b in zip(high, low)]


def block_targets():
    me = lax.axis_index(AXES)
    block = jnp.arange(128, dtype=jnp.int32)
    far = block >> 6
    core = ((me >> 5) & 1) ^ far
    target = me ^ (far * CORE)
    for bit in range(6):
        masks = order_of(0)[bit], order_of(1)[bit]
        move = (block >> (5 - bit)) & 1
        if bit >= 3:
            zero, one = coordinates(me, 0)[bit - 3], coordinates(me, 1)[bit - 3]
            move = move ^ (zero + core * (one - zero))
        target = target ^ (move * (masks[0] + core * (masks[1] - masks[0])))
    return target


def last_groups():
    groups = []
    for device in range(128):
        core = (device // CORE) % 2
        if not any(coordinates(device, core)):
            one, two, three = order_of(core)[3:]
            groups.append([device ^ (a * one) ^ (b * two) ^ (c * three) for a in (0, 1) for b in (0, 1) for c in (0, 1)])
    return groups


def total(terms):
    return sum((term.astype(jnp.float32) for term in terms[1:]), terms[0].astype(jnp.float32)).astype(jnp.bfloat16)


def split(terms, dim):
    shape = [term.reshape(2, 2, 2, 8, 8, -1) if term.ndim == 2 else term for term in terms]
    stay = [lax.index_in_dim(term, 0, dim, False) for term in shape]
    return stay, total([lax.index_in_dim(term, 1, dim, False) for term in shape])


def scatter_sum(first, beside):
    masks = list(zip(order_of(0), order_of(1)))
    left = [[bit for bit in range(3) if bit != part] for part in range(3)]
    parts, other = first, None
    for step in range(3):
        got = [exchange(go, masks[(part + step) % 3]) for part, (_, go) in enumerate(parts)]
        other, ready = beside[step]([go for _, go in parts], other)
        values = [stay + [come] for (stay, _), come in zip(parts, tie(got, ready))]
        if step < 2:
            parts = []
            for part, terms in enumerate(values):
                bit = (part + step + 1) % 3
                parts.append(split(terms, left[part].index(bit)))
                left[part].remove(bit)
    values = [total(terms) for terms in values]
    value = jnp.concatenate(values, -1)
    got = lax.all_to_all(value.reshape(64, -1), AXES, 0, 0, axis_index_groups=last_groups(), tiled=True)
    chosen = jnp.arange(64)[None, :] % 8 == jnp.arange(8)[:, None]
    return jnp.dot(chosen.astype(got.dtype), got, preferred_element_type=jnp.float32), other


def dot(a, b):
    return lax.dot_general(a, b, (((1,), (0,)), ((), ())), preferred_element_type=F32)


def dot_nt(a, b):
    return lax.dot_general(a, b, (((1,), (1,)), ((), ())), preferred_element_type=F32)


def dot_tn(a, b):
    return lax.dot_general(a, b, (((0,), (0,)), ((), ())), preferred_element_type=F32)


def normalize(rows):
    values = rows.astype(F32)
    center = values - jnp.mean(values, -1, keepdims=True)
    inverse = lax.rsqrt(jnp.mean(center * center, -1, keepdims=True) + epsilon)
    return center * inverse, inverse


def call(body, outs, ins, in_specs, out_specs, scratch, macs, steps=STEPS, room=30):
    size = sum(math.prod(x.shape) * x.dtype.itemsize for x in (*ins, *jax.tree.leaves(outs)))
    return pl.pallas_call(
        body,
        out_shape=outs,
        grid=(steps,),
        in_specs=in_specs,
        out_specs=out_specs,
        scratch_shapes=scratch,
        compiler_params=pltpu.CompilerParams(vmem_limit_bytes=room * 2**20),
        cost_estimate=pl.CostEstimate(flops=2 * macs, bytes_accessed=size, transcendentals=0),
    )(*ins)


def whole(*shape):
    return pl.BlockSpec(shape, lambda j: (0,) * len(shape))


def columns(rows):
    return pl.BlockSpec((rows, PAIR), lambda j: (0, j))


SCALAR = pl.BlockSpec(memory_space=pltpu.SMEM)
HELD = pl.BlockSpec(memory_space=pltpu.VMEM)
AFTER = pl.BlockSpec(memory_space=pl.ANY)


def one_hot(target, first, blocks):
    lane = lax.broadcasted_iota(jnp.int32, (8, D), 1) - lax.broadcasted_iota(jnp.int32, (8, D), 0)
    rows = [jnp.where(lane == 8 * target[first + block], 1.0, 0.0) for block in range(blocks)]
    return jnp.concatenate(rows, 0).astype(BF16)


def here():
    return lax.axis_index("tm") * ROWS


def tie_body(*refs):
    pass


def tie(values, after):
    return pl.pallas_call(
        tie_body,
        out_shape=[jax.ShapeDtypeStruct(value.shape, value.dtype) for value in values],
        in_specs=[AFTER] * (len(values) + 1),
        out_specs=[AFTER] * len(values),
        input_output_aliases={i: i for i in range(len(values))},
        compiler_params=pltpu.CompilerParams(vmem_limit_bytes=2**20),
        cost_estimate=pl.CostEstimate(flops=0, bytes_accessed=0, transcendentals=0),
    )(*values, after)


def pair_columns():
    return pl.ds(pl.multiple_of(pl.program_id(0) * PAIR, PAIR), PAIR)


def front_body(length, target, frames, grads, w_query, w_key, w_value, w_out, ordered, query, keys, values, d_mixed, hidden, masked):
    @pl.when(pl.program_id(0) == 0)
    def _():
        hidden[...] = normalize(frames[...])[0].astype(BF16)
        row = lax.broadcasted_iota(jnp.int32, (ROWS, D), 0) + here()
        masked[...] = jnp.where(row < length[0], grads[...].astype(F32), 0.0).astype(BF16)

    rows = hidden[...]
    now = pair_columns()
    d_mixed[:, now] = dot_nt(masked[...], w_out[...]).astype(BF16)
    query[:, now] = dot(rows, w_query[...]).astype(BF16)
    keys[:, now] = dot(rows, w_key[...]).astype(BF16)
    values[:, now] = dot(rows, w_value[...]).astype(BF16)
    ordered[now] = dot_nt(one_hot(target, pl.program_id(0) * (PAIR // 8), PAIR // 8), rows).astype(BF16)


def front(length, target, frames, grads, w_query, w_key, w_value, w_out):
    wide = jax.ShapeDtypeStruct((ROWS, D), BF16)
    return call(
        front_body,
        [jax.ShapeDtypeStruct((D, ROWS), BF16), wide, wide, wide, wide],
        (length, target, frames, grads, w_query, w_key, w_value, w_out),
        [SCALAR, SCALAR, whole(ROWS, D), whole(ROWS, D)] + [columns(D)] * 3 + [pl.BlockSpec((PAIR, D), lambda j: (j, 0))],
        [HELD] * 5,
        [pltpu.VMEM((ROWS, D), BF16)] * 2,
        5 * ROWS * D * D,
        room=ROOM[0],
    )


def attend_body(
    length, target, low, high, query_all, keys_all, values_all, d_mixed_all, w_key, w_value,
    grad_query_all, grad_key_all, grad_value_all, border_grads_all, ordered_border,
    hidden_border, key_value, pair, score_t, prob_t,
):
    scale = HDIM ** (-0.5)
    blocks = ROWS // WIN

    @pl.when(pl.program_id(0) == 0)
    def _():
        hidden_border[:WIN] = normalize(low[...])[0].astype(BF16)
        hidden_border[WIN:] = normalize(high[...])[0].astype(BF16)
        for part in range(4):
            rows = slice(part * PAIR, (part + 1) * PAIR)
            ordered_border[rows] = dot_nt(one_hot(target, part * (PAIR // 8), PAIR // 8), hidden_border[...]).astype(BF16)
        pair[...] = jnp.zeros_like(pair)
        outside = jnp.zeros((WIN, WIN), BF16)
        for ref in (score_t, prob_t):
            for head in range(2):
                for i in range(0, blocks, 2):
                    ref[head, (i + 3) * WIN : (i + 4) * WIN, i * WIN : (i + 1) * WIN] = outside
                    ref[head, i * WIN : (i + 1) * WIN, (i + 1) * WIN : (i + 2) * WIN] = outside

    query, keys, values, d_mixed = (
        ref.at[:, pair_columns()] for ref in (query_all, keys_all, values_all, d_mixed_all)
    )
    grad_query, grad_key, grad_value = (
        ref.at[:, pair_columns()] for ref in (grad_query_all, grad_key_all, grad_value_all)
    )
    border_grads = border_grads_all.at[:, :, pair_columns()]
    key_border = dot(hidden_border[...], w_key[...]).astype(BF16)
    value_border = dot(hidden_border[...], w_value[...]).astype(BF16)
    above = lax.broadcasted_iota(jnp.int32, (3 * WIN, WIN), 0)
    lane = lax.broadcasted_iota(jnp.int32, (1, WIN), 1)

    def lay_out(head):
        cols = slice(head * HDIM, (head + 1) * HDIM)
        for side, own, to in ((key_border, keys, slice(0, HDIM)), (value_border, values, slice(HDIM, PAIR))):
            key_value[head, :WIN, to] = side[:WIN, cols]
            key_value[head, WIN : WIN + ROWS, to] = own[:, cols]
            key_value[head, WIN + ROWS :, to] = side[WIN:, cols]
        for i in range(blocks):
            mine = slice(i * WIN, (i + 1) * WIN)
            pair[head, i * PAIR : i * PAIR + WIN, :HDIM] = query[mine, cols]
            pair[head, i * PAIR + WIN : (i + 1) * PAIR, HDIM:] = d_mixed[mine, cols]

    def products(head, i):
        return dot_nt(key_value[head, i * WIN : (i + 3) * WIN], pair[head, i * PAIR : (i + 1) * PAIR])

    def soften(head, i, both):
        mine = slice(i * WIN, (i + 1) * WIN)
        reach = slice(i * WIN, (i + 3) * WIN)
        first = (1 - i) * WIN - here()
        last = length[0] - here() + (1 - i) * WIN - 1
        allowed = (above >= jnp.maximum(lane, first)) & (above <= jnp.minimum(lane + 2 * WIN, last))
        scores = jnp.where(allowed, both[:, :WIN], masked_value)
        d_prob = both[:, WIN:]
        row_max = jnp.max(scores, 0, keepdims=True)
        expo = jnp.exp2((scores - row_max) * (scale * math.log2(math.e)))
        inverse_sum = 1.0 / jnp.sum(expo, 0, keepdims=True)
        row_delta = jnp.sum(expo * d_prob, 0, keepdims=True) * inverse_sum
        score_t[head, reach, mine] = (expo * (inverse_sum * scale) * (d_prob - row_delta)).astype(BF16)
        prob_t[head, reach, mine] = (expo * inverse_sum).astype(BF16)

    def query_grads(head, part):
        cols = slice(head * HDIM, (head + 1) * HDIM)
        mine = slice(part * PAIR, (part + 1) * PAIR)
        reach = slice(part * PAIR, part * PAIR + 2 * PAIR)
        grad_query[mine, cols] = dot_tn(score_t[head, reach, mine], key_value[head, reach, :HDIM]).astype(BF16)

    def key_grads(head, part):
        cols = slice(head * HDIM, (head + 1) * HDIM)
        here = slice(part * PAIR, (part + 1) * PAIR)
        near = slice(max(0, part - 1) * PAIR, min(2, part + 1) * PAIR)
        g_key = dot(score_t[head, here, near], query[near, cols]).astype(BF16)
        g_value = dot(prob_t[head, here, near], d_mixed[near, cols]).astype(BF16)
        if part == 0:
            border_grads[0, :WIN, cols], border_grads[1, :WIN, cols] = g_key[:WIN], g_value[:WIN]
            grad_key[:WIN, cols], grad_value[:WIN, cols] = g_key[WIN:], g_value[WIN:]
        elif part == 1:
            grad_key[WIN : WIN + PAIR, cols], grad_value[WIN : WIN + PAIR, cols] = g_key, g_value
        else:
            grad_key[ROWS - WIN :, cols], grad_value[ROWS - WIN :, cols] = g_key[:WIN], g_value[:WIN]
            border_grads[0, WIN:, cols], border_grads[1, WIN:, cols] = g_key[WIN:], g_value[WIN:]

    lay_out(0)
    lay_out(1)
    first = [products(0, i) for i in range(blocks)]
    second = []
    for i in range(blocks):
        soften(0, i, first[i])
        second.append(products(1, i))
    jobs = [(query_grads, 0), (query_grads, 1), (key_grads, 0), (key_grads, 1), (key_grads, 2)]
    for i in range(blocks):
        soften(1, i, second[i])
        for job, part in jobs[i : i + 1] if i < 3 else jobs[3:]:
            job(0, part)
    for job, part in jobs:
        job(1, part)


def attend(length, target, low, high, query, keys, values, d_mixed, w_key, w_value):
    own = jax.ShapeDtypeStruct((ROWS, D), BF16)
    reach = ROWS + 2 * WIN
    return call(
        attend_body,
        [own] * 3 + [jax.ShapeDtypeStruct((2, 2 * WIN, D), BF16), jax.ShapeDtypeStruct((D, 2 * WIN), BF16)],
        (length, target, low, high, query, keys, values, d_mixed, w_key, w_value),
        [SCALAR, SCALAR, whole(WIN, D), whole(WIN, D)] + [HELD] * 4 + [columns(D)] * 2,
        [HELD] * 5,
        [
            pltpu.VMEM((2 * WIN, D), BF16),
            pltpu.VMEM((2, reach, PAIR), BF16),
            pltpu.VMEM((2, 2 * ROWS, PAIR), BF16),
            pltpu.VMEM((2, reach, ROWS), BF16),
            pltpu.VMEM((2, reach, ROWS), BF16),
        ],
        D * D * WIN * 4 + 10 * 4 * 3 * HEADS * WIN**3,
        room=ROOM[2],
    )


def project_body(ordered, grad, kept, sent):
    half = D // 2
    columns = grad[:, pair_columns()]
    sent[:, pair_columns()] = dot(ordered[half:], columns).astype(BF16)
    kept[:, pair_columns()] = dot(ordered[:half], columns).astype(BF16)


def project_border_body(part, ordered, grad, ordered_border, border_grads, *rest):
    kept, sent = rest[-2:]
    half = D // 2
    columns, border_columns = grad[:, pair_columns()], border_grads[part - 1, :, pair_columns()]
    for out, rows in ((sent, slice(half, D)), (kept, slice(0, half))):
        out[:, pair_columns()] = (dot(ordered[rows], columns) + dot(ordered_border[rows], border_columns)).astype(BF16)


def project(part, *ins):
    half = jax.ShapeDtypeStruct((D // 2, D), BF16)
    body = functools.partial(project_border_body, part) if part else project_body
    specs = [HELD] * min(len(ins), 4) + [AFTER] * (len(ins) - 4)
    return call(body, [half] * 2, ins, specs, [HELD] * 2, [], D * D * (ROWS + 2 * WIN), room=20)


def back_body(grad_query, grad_key, grad_value, w_query, w_key, w_value, *rest):
    total = rest[-1]
    total[:, pair_columns()] = (
        dot_nt(grad_query[...], w_query[...]) + dot_nt(grad_key[...], w_key[...]) + dot_nt(grad_value[...], w_value[...])
    )


def rows_of(columns):
    return pl.BlockSpec((PAIR, columns), lambda j: (j, 0))


def back(*ins):
    return call(
        back_body,
        jax.ShapeDtypeStruct((ROWS, D), F32),
        ins,
        [HELD] * 3 + [rows_of(D)] * 3 + [AFTER] * 3,
        HELD,
        [],
        3 * ROWS * D * D,
        room=24,
    )


def back_border_body(grads, w_key, w_value, *rest):
    sides = rest[-1]
    sides[:, pair_columns()] = (dot_nt(grads[0], w_key[...]) + dot_nt(grads[1], w_value[...])).astype(BF16)


def back_border(*ins):
    return call(
        back_border_body,
        jax.ShapeDtypeStruct((2 * WIN, D), BF16),
        ins,
        [HELD] + [rows_of(D)] * 2 + [AFTER] * 3,
        HELD,
        [],
        4 * WIN * D * D,
        room=16,
    )


def finish_body(frames, grads, d_hidden, near, after, out):
    normed, inverse = normalize(frames[...])
    part = pl.program_id(0)
    inner = jnp.logical_and(part > 0, part < STEPS - 1)
    d_rows = d_hidden[...] + jnp.where(inner, 0.0, near[...].astype(F32))
    mean_grad = jnp.mean(d_rows, -1, keepdims=True)
    mean_cross = jnp.mean(d_rows * normed, -1, keepdims=True)
    out[...] = (grads[...].astype(F32) + inverse * (d_rows - mean_grad - normed * mean_cross)).astype(BF16)


def finish(frames, grads, d_hidden, near, after):
    block = pl.BlockSpec((WIN, D), lambda j: (j, 0))
    return call(
        finish_body,
        jax.ShapeDtypeStruct((ROWS, D), BF16),
        (frames, grads, d_hidden, near, after),
        [block] * 3 + [pl.BlockSpec((WIN, D), lambda j: (j // (STEPS - 1), 0)), AFTER],
        block,
        [],
        ROWS * D * 16,
        room=16,
    )


def swap(first, last, pairs):
    even = lax.axis_index("tm") % 2 == 0
    return send(jnp.where(even, last, first) if pairs == 0 else jnp.where(even, first, last), pairs)


def send(rows, pairs):
    count = lax.axis_size("tm")
    if pairs == 0:
        return lax.ppermute(rows, "tm", [(i, i ^ 1) for i in range(count)])
    return lax.ppermute(rows, "tm", [(i, i + 1 if i % 2 else i - 1) for i in range(1, count - 1)])


def choose_body(sides, *rest):
    within, across = rest[-2:]
    even = lax.axis_index("tm") % 2 == 0

    @pl.when(even)
    def _():
        within[...] = sides[WIN:]
        across[...] = sides[:WIN]

    @pl.when(jnp.logical_not(even))
    def _():
        within[...] = sides[:WIN]
        across[...] = sides[WIN:]


def choose(sides, *after):
    half = jax.ShapeDtypeStruct((WIN, D), BF16)
    return call(choose_body, [half] * 2, (sides, *after), [whole(2 * WIN, D)] + [AFTER] * 3, [whole(WIN, D)] * 2, [], 0, steps=1, room=8)


def in_order(within, across):
    even = lax.axis_index("tm") % 2 == 0
    return jnp.where(even, across, within), jnp.where(even, within, across)


def in_hbm(*arrays):
    return [pltpu.with_memory_space_constraint(array, pltpu.HBM) for array in arrays]


def shards(frames, cotangent, lengths, w_query, w_key, w_value, w_out):
    rows, grads = frames[0], cotangent[0]
    w_query, w_key, w_value, w_out = in_hbm(w_query, w_key, w_value, w_out)
    top, end = rows[:WIN], rows[ROWS - WIN :]
    within, across = swap(top, end, 0), swap(top, end, 1)
    target = block_targets()
    ordered, query, keys, values, d_mixed = front(lengths, target, *in_hbm(rows, grads), w_query, w_key, w_value, w_out)
    low, high = in_order(within, across)
    grad_query, grad_key, grad_value, border_grads, ordered_border = attend(
        lengths, target, low, high, query, keys, values, d_mixed, w_key, w_value
    )
    parts = []
    for part, ins in enumerate(
        (
            (ordered, grad_query),
            (ordered, grad_key, ordered_border, border_grads),
            (ordered, grad_value, ordered_border, border_grads),
        )
    ):
        kept, sent = project(part, *ins, *(parts[0][1:] if part == 2 else ()))
        parts.append(split([kept, exchange(sent, (CORE, CORE))], part))

    def first(after, _):
        d_hidden = back(grad_query, grad_key, grad_value, w_query, w_key, w_value, *after)
        return d_hidden, d_hidden

    def second(after, d_hidden):
        sides = back_border(border_grads, w_key, w_value, *after)
        return (d_hidden, sides), sides

    def third(after, before):
        d_hidden, sides = before
        within, across = choose(sides, *after)
        return (d_hidden, send(within, 0), send(across, 1)), within

    weight_part, (d_hidden, within, across) = scatter_sum(parts, (first, second, third))
    grad_frames = finish(rows, grads, d_hidden, jnp.concatenate(in_order(within, across)), parts[2][1])
    return (grad_frames[None], weight_part)


def solution(mesh):
    placed = (P("rec", "tm", None), P("rec", "tm", None), P("rec"), P(), P(), P(), P())
    return jax.shard_map(
        shards,
        mesh=mesh,
        in_specs=placed,
        out_specs=(P("rec", "tm", None), P(("rec", "tm"), None)),
        check_vma=False,
    )
```

```python
import functools
import math

import jax
import jax.numpy as jnp
from jax import lax
from jax.experimental import pallas as pl
from jax.experimental.pallas import tpu as pltpu
from jax.sharding import PartitionSpec as P

HEADS = 8
WIN = 128
HDIM = 128
ROWS = 512
D = 1024
PAIR = 2 * HDIM
STEPS = HEADS // 2
epsilon = 1e-05
masked_value = -1e30
F32 = jnp.float32
BF16 = jnp.bfloat16
ROOM = (30, 30, 30, 30)

AXES = ("rec", "tm")
CORE = 32
NEAR = ((16, 4, 1), (80, 12, 3))


def order_of(core):
    return NEAR[core] + NEAR[1 - core]


def exchange(value, masks):
    count = lax.axis_size(AXES)
    pairs = [(i, i ^ masks[(i // CORE) % 2]) for i in range(count)]
    return lax.ppermute(value, AXES, pairs)


def coordinates(device, core):
    high = [(device >> bit) & 1 for bit in (6, 3, 1)]
    low = [(device >> bit) & 1 for bit in (4, 2, 0)]
    return high if core == 0 else [a ^ b for a, b in zip(high, low)]


def block_targets():
    me = lax.axis_index(AXES)
    block = jnp.arange(128, dtype=jnp.int32)
    far = block >> 6
    core = ((me >> 5) & 1) ^ far
    target = me ^ (far * CORE)
    for bit in range(6):
        masks = order_of(0)[bit], order_of(1)[bit]
        move = (block >> (5 - bit)) & 1
        if bit >= 3:
            zero, one = coordinates(me, 0)[bit - 3], coordinates(me, 1)[bit - 3]
            move = move ^ (zero + core * (one - zero))
        target = target ^ (move * (masks[0] + core * (masks[1] - masks[0])))
    return target


def last_groups():
    groups = []
    for device in range(128):
        core = (device // CORE) % 2
        if not any(coordinates(device, core)):
            one, two, three = order_of(core)[3:]
            groups.append([device ^ (a * one) ^ (b * two) ^ (c * three) for a in (0, 1) for b in (0, 1) for c in (0, 1)])
    return groups


def total(terms):
    return sum((term.astype(jnp.float32) for term in terms[1:]), terms[0].astype(jnp.float32)).astype(jnp.bfloat16)


def split(terms, dim):
    shape = [term.reshape(2, 2, 2, 8, 8, -1) if term.ndim == 2 else term for term in terms]
    stay = [lax.index_in_dim(term, 0, dim, False) for term in shape]
    return stay, total([lax.index_in_dim(term, 1, dim, False) for term in shape])


def scatter_sum(first, beside):
    masks = list(zip(order_of(0), order_of(1)))
    left = [[bit for bit in range(3) if bit != part] for part in range(3)]
    parts, other = first, None
    for step in range(3):
        got = [exchange(go, masks[(part + step) % 3]) for part, (_, go) in enumerate(parts)]
        other, ready = beside[step]([go for _, go in parts], other)
        values = [stay + [come] for (stay, _), come in zip(parts, tie(got, ready))]
        if step < 2:
            parts = []
            for part, terms in enumerate(values):
                bit = (part + step + 1) % 3
                parts.append(split(terms, left[part].index(bit)))
                left[part].remove(bit)
    values = [total(terms) for terms in values]
    value = jnp.concatenate(values, -1)
    got = lax.all_to_all(value.reshape(64, -1), AXES, 0, 0, axis_index_groups=last_groups(), tiled=True)
    chosen = jnp.arange(64)[None, :] % 8 == jnp.arange(8)[:, None]
    return jnp.dot(chosen.astype(got.dtype), got, preferred_element_type=jnp.float32), other


def dot(a, b):
    return lax.dot_general(a, b, (((1,), (0,)), ((), ())), preferred_element_type=F32)


def dot_nt(a, b):
    return lax.dot_general(a, b, (((1,), (1,)), ((), ())), preferred_element_type=F32)


def dot_tn(a, b):
    return lax.dot_general(a, b, (((0,), (0,)), ((), ())), preferred_element_type=F32)


def normalize(rows):
    values = rows.astype(F32)
    center = values - jnp.mean(values, -1, keepdims=True)
    inverse = lax.rsqrt(jnp.mean(center * center, -1, keepdims=True) + epsilon)
    return center * inverse, inverse


def call(body, outs, ins, in_specs, out_specs, scratch, macs, steps=STEPS, room=30):
    size = sum(math.prod(x.shape) * x.dtype.itemsize for x in (*ins, *jax.tree.leaves(outs)))
    return pl.pallas_call(
        body,
        out_shape=outs,
        grid=(steps,),
        in_specs=in_specs,
        out_specs=out_specs,
        scratch_shapes=scratch,
        compiler_params=pltpu.CompilerParams(vmem_limit_bytes=room * 2**20),
        cost_estimate=pl.CostEstimate(flops=2 * macs, bytes_accessed=size, transcendentals=0),
    )(*ins)


def whole(*shape):
    return pl.BlockSpec(shape, lambda j: (0,) * len(shape))


def columns(rows):
    return pl.BlockSpec((rows, PAIR), lambda j: (0, j))


SCALAR = pl.BlockSpec(memory_space=pltpu.SMEM)
HELD = pl.BlockSpec(memory_space=pltpu.VMEM)
AFTER = pl.BlockSpec(memory_space=pl.ANY)


def one_hot(target, first, blocks):
    lane = lax.broadcasted_iota(jnp.int32, (8, D), 1) - lax.broadcasted_iota(jnp.int32, (8, D), 0)
    rows = [jnp.where(lane == 8 * target[first + block], 1.0, 0.0) for block in range(blocks)]
    return jnp.concatenate(rows, 0).astype(BF16)


def here():
    return lax.axis_index("tm") * ROWS


def tie_body(*refs):
    pass


def tie(values, after):
    return pl.pallas_call(
        tie_body,
        out_shape=[jax.ShapeDtypeStruct(value.shape, value.dtype) for value in values],
        in_specs=[AFTER] * (len(values) + 1),
        out_specs=[AFTER] * len(values),
        input_output_aliases={i: i for i in range(len(values))},
        compiler_params=pltpu.CompilerParams(vmem_limit_bytes=2**20),
        cost_estimate=pl.CostEstimate(flops=0, bytes_accessed=0, transcendentals=0),
    )(*values, after)


def pair_columns():
    return pl.ds(pl.multiple_of(pl.program_id(0) * PAIR, PAIR), PAIR)


def front_body(length, target, frames, grads, w_query, w_key, w_value, w_out, ordered, query, keys, values, d_mixed, hidden, masked):
    @pl.when(pl.program_id(0) == 0)
    def _():
        hidden[...] = normalize(frames[...])[0].astype(BF16)
        row = lax.broadcasted_iota(jnp.int32, (ROWS, D), 0) + here()
        masked[...] = jnp.where(row < length[0], grads[...].astype(F32), 0.0).astype(BF16)

    rows = hidden[...]
    now = pair_columns()
    d_mixed[:, now] = dot_nt(masked[...], w_out[...]).astype(BF16)
    query[:, now] = dot(rows, w_query[...]).astype(BF16)
    keys[:, now] = dot(rows, w_key[...]).astype(BF16)
    values[:, now] = dot(rows, w_value[...]).astype(BF16)
    ordered[now] = dot_nt(one_hot(target, pl.program_id(0) * (PAIR // 8), PAIR // 8), rows).astype(BF16)


def front(length, target, frames, grads, w_query, w_key, w_value, w_out):
    wide = jax.ShapeDtypeStruct((ROWS, D), BF16)
    return call(
        front_body,
        [jax.ShapeDtypeStruct((D, ROWS), BF16), wide, wide, wide, wide],
        (length, target, frames, grads, w_query, w_key, w_value, w_out),
        [SCALAR, SCALAR, whole(ROWS, D), whole(ROWS, D)] + [columns(D)] * 3 + [pl.BlockSpec((PAIR, D), lambda j: (j, 0))],
        [HELD] * 5,
        [pltpu.VMEM((ROWS, D), BF16)] * 2,
        5 * ROWS * D * D,
        room=ROOM[0],
    )


def attend_body(
    length, target, low, high, query_all, keys_all, values_all, d_mixed_all, w_key, w_value,
    grad_query_all, grad_key_all, grad_value_all, border_grads_all, ordered_border,
    hidden_border, key_value, pair, score_t, prob_t,
):
    scale = HDIM ** (-0.5)
    blocks = ROWS // WIN

    @pl.when(pl.program_id(0) == 0)
    def _():
        hidden_border[:WIN] = normalize(low[...])[0].astype(BF16)
        hidden_border[WIN:] = normalize(high[...])[0].astype(BF16)
        for part in range(4):
            rows = slice(part * PAIR, (part + 1) * PAIR)
            ordered_border[rows] = dot_nt(one_hot(target, part * (PAIR // 8), PAIR // 8), hidden_border[...]).astype(BF16)
        pair[...] = jnp.zeros_like(pair)
        outside = jnp.zeros((WIN, WIN), BF16)
        for ref in (score_t, prob_t):
            for head in range(2):
                for i in range(0, blocks, 2):
                    ref[head, (i + 3) * WIN : (i + 4) * WIN, i * WIN : (i + 1) * WIN] = outside
                    ref[head, i * WIN : (i + 1) * WIN, (i + 1) * WIN : (i + 2) * WIN] = outside

    query, keys, values, d_mixed = (
        ref.at[:, pair_columns()] for ref in (query_all, keys_all, values_all, d_mixed_all)
    )
    grad_query, grad_key, grad_value = (
        ref.at[:, pair_columns()] for ref in (grad_query_all, grad_key_all, grad_value_all)
    )
    border_grads = border_grads_all.at[:, :, pair_columns()]
    key_border = dot(hidden_border[...], w_key[...]).astype(BF16)
    value_border = dot(hidden_border[...], w_value[...]).astype(BF16)
    above = lax.broadcasted_iota(jnp.int32, (3 * WIN, WIN), 0)
    lane = lax.broadcasted_iota(jnp.int32, (1, WIN), 1)

    def lay_out(head):
        cols = slice(head * HDIM, (head + 1) * HDIM)
        for side, own, to in ((key_border, keys, slice(0, HDIM)), (value_border, values, slice(HDIM, PAIR))):
            key_value[head, :WIN, to] = side[:WIN, cols]
            key_value[head, WIN : WIN + ROWS, to] = own[:, cols]
            key_value[head, WIN + ROWS :, to] = side[WIN:, cols]
        for i in range(blocks):
            mine = slice(i * WIN, (i + 1) * WIN)
            pair[head, i * PAIR : i * PAIR + WIN, :HDIM] = query[mine, cols]
            pair[head, i * PAIR + WIN : (i + 1) * PAIR, HDIM:] = d_mixed[mine, cols]

    def products(head, i):
        return dot_nt(key_value[head, i * WIN : (i + 3) * WIN], pair[head, i * PAIR : (i + 1) * PAIR])

    def soften(head, i, both):
        mine = slice(i * WIN, (i + 1) * WIN)
        reach = slice(i * WIN, (i + 3) * WIN)
        first = (1 - i) * WIN - here()
        last = length[0] - here() + (1 - i) * WIN - 1
        allowed = (above >= jnp.maximum(lane, first)) & (above <= jnp.minimum(lane + 2 * WIN, last))
        scores = jnp.where(allowed, both[:, :WIN], masked_value)
        d_prob = both[:, WIN:]
        row_max = jnp.max(scores, 0, keepdims=True)
        expo = jnp.exp2((scores - row_max) * (scale * math.log2(math.e)))
        inverse_sum = 1.0 / jnp.sum(expo, 0, keepdims=True)
        row_delta = jnp.sum(expo * d_prob, 0, keepdims=True) * inverse_sum
        score_t[head, reach, mine] = (expo * (inverse_sum * scale) * (d_prob - row_delta)).astype(BF16)
        prob_t[head, reach, mine] = (expo * inverse_sum).astype(BF16)

    def query_grads(head, part):
        cols = slice(head * HDIM, (head + 1) * HDIM)
        mine = slice(part * PAIR, (part + 1) * PAIR)
        reach = slice(part * PAIR, part * PAIR + 2 * PAIR)
        grad_query[mine, cols] = dot_tn(score_t[head, reach, mine], key_value[head, reach, :HDIM]).astype(BF16)

    def key_grads(head, part):
        cols = slice(head * HDIM, (head + 1) * HDIM)
        here = slice(part * PAIR, (part + 1) * PAIR)
        near = slice(max(0, part - 1) * PAIR, min(2, part + 1) * PAIR)
        g_key = dot(score_t[head, here, near], query[near, cols]).astype(BF16)
        g_value = dot(prob_t[head, here, near], d_mixed[near, cols]).astype(BF16)
        if part == 0:
            border_grads[0, :WIN, cols], border_grads[1, :WIN, cols] = g_key[:WIN], g_value[:WIN]
            grad_key[:WIN, cols], grad_value[:WIN, cols] = g_key[WIN:], g_value[WIN:]
        elif part == 1:
            grad_key[WIN : WIN + PAIR, cols], grad_value[WIN : WIN + PAIR, cols] = g_key, g_value
        else:
            grad_key[ROWS - WIN :, cols], grad_value[ROWS - WIN :, cols] = g_key[:WIN], g_value[:WIN]
            border_grads[0, WIN:, cols], border_grads[1, WIN:, cols] = g_key[WIN:], g_value[WIN:]

    lay_out(0)
    lay_out(1)
    first = [products(0, i) for i in range(blocks)]
    second = []
    for i in range(blocks):
        soften(0, i, first[i])
        second.append(products(1, i))
    jobs = [(query_grads, 0), (query_grads, 1), (key_grads, 0), (key_grads, 1), (key_grads, 2)]
    for i in range(blocks):
        soften(1, i, second[i])
        for job, part in jobs[i : i + 1] if i < 3 else jobs[3:]:
            job(0, part)
    for job, part in jobs:
        job(1, part)


def attend(length, target, low, high, query, keys, values, d_mixed, w_key, w_value):
    own = jax.ShapeDtypeStruct((ROWS, D), BF16)
    reach = ROWS + 2 * WIN
    return call(
        attend_body,
        [own] * 3 + [jax.ShapeDtypeStruct((2, 2 * WIN, D), BF16), jax.ShapeDtypeStruct((D, 2 * WIN), BF16)],
        (length, target, low, high, query, keys, values, d_mixed, w_key, w_value),
        [SCALAR, SCALAR, whole(WIN, D), whole(WIN, D)] + [HELD] * 4 + [columns(D)] * 2,
        [HELD] * 5,
        [
            pltpu.VMEM((2 * WIN, D), BF16),
            pltpu.VMEM((2, reach, PAIR), BF16),
            pltpu.VMEM((2, 2 * ROWS, PAIR), BF16),
            pltpu.VMEM((2, reach, ROWS), BF16),
            pltpu.VMEM((2, reach, ROWS), BF16),
        ],
        D * D * WIN * 4 + 10 * 4 * 3 * HEADS * WIN**3,
        room=ROOM[2],
    )


def project_body(ordered, grad, kept, sent):
    half = D // 2
    for now in (slice(j * PAIR, (j + 1) * PAIR) for j in range(STEPS)):
        sent[:, now] = dot(ordered[half:], grad[:, now]).astype(BF16)
        kept[:, now] = dot(ordered[:half], grad[:, now]).astype(BF16)


def project_border_body(part, ordered, grad, ordered_border, border_grads, *rest):
    kept, sent = rest[-2:]
    half = D // 2
    for now in (slice(j * PAIR, (j + 1) * PAIR) for j in range(STEPS)):
        for out, rows in ((sent, slice(half, D)), (kept, slice(0, half))):
            own, border = dot(ordered[rows], grad[:, now]), dot(ordered_border[rows], border_grads[part - 1, :, now])
            out[:, now] = (own + border).astype(BF16)


def project(part, *ins):
    half = jax.ShapeDtypeStruct((D // 2, D), BF16)
    body = functools.partial(project_border_body, part) if part else project_body
    specs = [HELD] * min(len(ins), 4) + [AFTER] * (len(ins) - 4)
    return call(body, [half] * 2, ins, specs, [HELD] * 2, [], D * D * (ROWS + 2 * WIN), steps=1, room=20)


def back_body(grad_query, grad_key, grad_value, w_query, w_key, w_value, *rest):
    total = rest[-1]
    total[:, pair_columns()] = (
        dot_nt(grad_query[...], w_query[...]) + dot_nt(grad_key[...], w_key[...]) + dot_nt(grad_value[...], w_value[...])
    )


def rows_of(columns):
    return pl.BlockSpec((PAIR, columns), lambda j: (j, 0))


def back(*ins):
    return call(
        back_body,
        jax.ShapeDtypeStruct((ROWS, D), F32),
        ins,
        [HELD] * 3 + [rows_of(D)] * 3 + [AFTER] * 3,
        HELD,
        [],
        3 * ROWS * D * D,
        room=24,
    )


def back_border_body(grads, w_key, w_value, *rest):
    sides = rest[-1]
    sides[:, pair_columns()] = (dot_nt(grads[0], w_key[...]) + dot_nt(grads[1], w_value[...])).astype(BF16)


def back_border(*ins):
    return call(
        back_border_body,
        jax.ShapeDtypeStruct((2 * WIN, D), BF16),
        ins,
        [HELD] + [rows_of(D)] * 2 + [AFTER] * 3,
        HELD,
        [],
        4 * WIN * D * D,
        room=16,
    )


def finish_body(frames, grads, d_hidden, near, after, out):
    normed, inverse = normalize(frames[...])
    part = pl.program_id(0)
    inner = jnp.logical_and(part > 0, part < STEPS - 1)
    d_rows = d_hidden[...] + jnp.where(inner, 0.0, near[...].astype(F32))
    mean_grad = jnp.mean(d_rows, -1, keepdims=True)
    mean_cross = jnp.mean(d_rows * normed, -1, keepdims=True)
    out[...] = (grads[...].astype(F32) + inverse * (d_rows - mean_grad - normed * mean_cross)).astype(BF16)


def finish(frames, grads, d_hidden, near, after):
    block = pl.BlockSpec((WIN, D), lambda j: (j, 0))
    return call(
        finish_body,
        jax.ShapeDtypeStruct((ROWS, D), BF16),
        (frames, grads, d_hidden, near, after),
        [block] * 3 + [pl.BlockSpec((WIN, D), lambda j: (j // (STEPS - 1), 0)), AFTER],
        block,
        [],
        ROWS * D * 16,
        room=16,
    )


def swap(first, last, pairs):
    even = lax.axis_index("tm") % 2 == 0
    return send(jnp.where(even, last, first) if pairs == 0 else jnp.where(even, first, last), pairs)


def send(rows, pairs):
    count = lax.axis_size("tm")
    if pairs == 0:
        return lax.ppermute(rows, "tm", [(i, i ^ 1) for i in range(count)])
    return lax.ppermute(rows, "tm", [(i, i + 1 if i % 2 else i - 1) for i in range(1, count - 1)])


def choose_body(sides, *rest):
    within, across = rest[-2:]
    even = lax.axis_index("tm") % 2 == 0

    @pl.when(even)
    def _():
        within[...] = sides[WIN:]
        across[...] = sides[:WIN]

    @pl.when(jnp.logical_not(even))
    def _():
        within[...] = sides[:WIN]
        across[...] = sides[WIN:]


def choose(sides, *after):
    half = jax.ShapeDtypeStruct((WIN, D), BF16)
    return call(choose_body, [half] * 2, (sides, *after), [whole(2 * WIN, D)] + [AFTER] * 3, [whole(WIN, D)] * 2, [], 0, steps=1, room=8)


def in_order(within, across):
    even = lax.axis_index("tm") % 2 == 0
    return jnp.where(even, across, within), jnp.where(even, within, across)


def in_hbm(*arrays):
    return [pltpu.with_memory_space_constraint(array, pltpu.HBM) for array in arrays]


def shards(frames, cotangent, lengths, w_query, w_key, w_value, w_out):
    rows, grads = frames[0], cotangent[0]
    w_query, w_key, w_value, w_out = in_hbm(w_query, w_key, w_value, w_out)
    top, end = rows[:WIN], rows[ROWS - WIN :]
    within, across = swap(top, end, 0), swap(top, end, 1)
    target = block_targets()
    ordered, query, keys, values, d_mixed = front(lengths, target, *in_hbm(rows, grads), w_query, w_key, w_value, w_out)
    low, high = in_order(within, across)
    grad_query, grad_key, grad_value, border_grads, ordered_border = attend(
        lengths, target, low, high, query, keys, values, d_mixed, w_key, w_value
    )
    parts = []
    for part, ins in enumerate(
        (
            (ordered, grad_query),
            (ordered, grad_key, ordered_border, border_grads),
            (ordered, grad_value, ordered_border, border_grads),
        )
    ):
        kept, sent = project(part, *ins, *(parts[0][1:] if part == 2 else ()))
        parts.append(split([kept, exchange(sent, (CORE, CORE))], part))

    def first(after, _):
        d_hidden = back(grad_query, grad_key, grad_value, w_query, w_key, w_value, *after)
        return d_hidden, d_hidden

    def second(after, d_hidden):
        sides = back_border(border_grads, w_key, w_value, *after)
        return (d_hidden, sides), sides

    def third(after, before):
        d_hidden, sides = before
        within, across = choose(sides, *after)
        return (d_hidden, send(within, 0), send(across, 1)), within

    weight_part, (d_hidden, within, across) = scatter_sum(parts, (first, second, third))
    grad_frames = finish(rows, grads, d_hidden, jnp.concatenate(in_order(within, across)), parts[2][1])
    return (grad_frames[None], weight_part)


def solution(mesh):
    placed = (P("rec", "tm", None), P("rec", "tm", None), P("rec"), P(), P(), P(), P())
    return jax.shard_map(
        shards,
        mesh=mesh,
        in_specs=placed,
        out_specs=(P("rec", "tm", None), P(("rec", "tm"), None)),
        check_vma=False,
    )
```

```python
import functools
import math

import jax
import jax.numpy as jnp
from jax import lax
from jax.experimental import pallas as pl
from jax.experimental.pallas import tpu as pltpu
from jax.sharding import PartitionSpec as P

HEADS = 8
WIN = 128
HDIM = 128
ROWS = 512
D = 1024
PAIR = 2 * HDIM
STEPS = HEADS // 2
epsilon = 1e-05
masked_value = -1e30
F32 = jnp.float32
BF16 = jnp.bfloat16
ROOM = (30, 30, 30, 30)

AXES = ("rec", "tm")
CORE = 32
NEAR = ((16, 4, 1), (80, 12, 3))


def order_of(core):
    return NEAR[core] + NEAR[1 - core]


def exchange(value, masks):
    count = lax.axis_size(AXES)
    pairs = [(i, i ^ masks[(i // CORE) % 2]) for i in range(count)]
    return lax.ppermute(value, AXES, pairs)


def coordinates(device, core):
    high = [(device >> bit) & 1 for bit in (6, 3, 1)]
    low = [(device >> bit) & 1 for bit in (4, 2, 0)]
    return high if core == 0 else [a ^ b for a, b in zip(high, low)]


def block_targets():
    me = lax.axis_index(AXES)
    block = jnp.arange(128, dtype=jnp.int32)
    far = block >> 6
    core = ((me >> 5) & 1) ^ far
    target = me ^ (far * CORE)
    for bit in range(6):
        masks = order_of(0)[bit], order_of(1)[bit]
        move = (block >> (5 - bit)) & 1
        if bit >= 3:
            zero, one = coordinates(me, 0)[bit - 3], coordinates(me, 1)[bit - 3]
            move = move ^ (zero + core * (one - zero))
        target = target ^ (move * (masks[0] + core * (masks[1] - masks[0])))
    return target


def last_groups():
    groups = []
    for device in range(128):
        core = (device // CORE) % 2
        if not any(coordinates(device, core)):
            one, two, three = order_of(core)[3:]
            groups.append([device ^ (a * one) ^ (b * two) ^ (c * three) for a in (0, 1) for b in (0, 1) for c in (0, 1)])
    return groups


def total(terms):
    return sum((term.astype(jnp.float32) for term in terms[1:]), terms[0].astype(jnp.float32)).astype(jnp.bfloat16)


def split(terms, dim):
    shape = [term.reshape(2, 2, 2, 8, 8, -1) if term.ndim == 2 else term for term in terms]
    stay = [lax.index_in_dim(term, 0, dim, False) for term in shape]
    return stay, total([lax.index_in_dim(term, 1, dim, False) for term in shape])


def scatter_sum(first, beside):
    masks = list(zip(order_of(0), order_of(1)))
    left = [[bit for bit in range(3) if bit != part] for part in range(3)]
    parts, other = first, None
    for step in range(3):
        got = [exchange(go, masks[(part + step) % 3]) for part, (_, go) in enumerate(parts)]
        other, ready = beside[step]([go for _, go in parts], other)
        values = [stay + [come] for (stay, _), come in zip(parts, tie(got, ready))]
        if step < 2:
            parts = []
            for part, terms in enumerate(values):
                bit = (part + step + 1) % 3
                parts.append(split(terms, left[part].index(bit)))
                left[part].remove(bit)
    values = [total(terms) for terms in values]
    value = jnp.concatenate(values, -1)
    got = lax.all_to_all(value.reshape(64, -1), AXES, 0, 0, axis_index_groups=last_groups(), tiled=True)
    chosen = jnp.arange(64)[None, :] % 8 == jnp.arange(8)[:, None]
    return jnp.dot(chosen.astype(got.dtype), got, preferred_element_type=jnp.float32), other


def dot(a, b):
    return lax.dot_general(a, b, (((1,), (0,)), ((), ())), preferred_element_type=F32)


def dot_nt(a, b):
    return lax.dot_general(a, b, (((1,), (1,)), ((), ())), preferred_element_type=F32)


def dot_tn(a, b):
    return lax.dot_general(a, b, (((0,), (0,)), ((), ())), preferred_element_type=F32)


def normalize(rows):
    values = rows.astype(F32)
    center = values - jnp.mean(values, -1, keepdims=True)
    inverse = lax.rsqrt(jnp.mean(center * center, -1, keepdims=True) + epsilon)
    return center * inverse, inverse


def call(body, outs, ins, in_specs, out_specs, scratch, macs, steps=STEPS, room=30):
    size = sum(math.prod(x.shape) * x.dtype.itemsize for x in (*ins, *jax.tree.leaves(outs)))
    return pl.pallas_call(
        body,
        out_shape=outs,
        grid=(steps,),
        in_specs=in_specs,
        out_specs=out_specs,
        scratch_shapes=scratch,
        compiler_params=pltpu.CompilerParams(vmem_limit_bytes=room * 2**20),
        cost_estimate=pl.CostEstimate(flops=2 * macs, bytes_accessed=size, transcendentals=0),
    )(*ins)


def whole(*shape):
    return pl.BlockSpec(shape, lambda j: (0,) * len(shape))


def columns(rows):
    return pl.BlockSpec((rows, PAIR), lambda j: (0, j))


SCALAR = pl.BlockSpec(memory_space=pltpu.SMEM)
HELD = pl.BlockSpec(memory_space=pltpu.VMEM)
AFTER = pl.BlockSpec(memory_space=pl.ANY)


def one_hot(target, first, blocks):
    lane = lax.broadcasted_iota(jnp.int32, (8, D), 1) - lax.broadcasted_iota(jnp.int32, (8, D), 0)
    rows = [jnp.where(lane == 8 * target[first + block], 1.0, 0.0) for block in range(blocks)]
    return jnp.concatenate(rows, 0).astype(BF16)


def here():
    return lax.axis_index("tm") * ROWS


def tie_body(*refs):
    pass


def tie(values, after):
    return pl.pallas_call(
        tie_body,
        out_shape=[jax.ShapeDtypeStruct(value.shape, value.dtype) for value in values],
        in_specs=[AFTER] * (len(values) + 1),
        out_specs=[AFTER] * len(values),
        input_output_aliases={i: i for i in range(len(values))},
        compiler_params=pltpu.CompilerParams(vmem_limit_bytes=2**20),
        cost_estimate=pl.CostEstimate(flops=0, bytes_accessed=0, transcendentals=0),
    )(*values, after)


def pair_columns():
    return pl.ds(pl.multiple_of(pl.program_id(0) * PAIR, PAIR), PAIR)


def front_body(length, target, frames, grads, w_query, w_key, w_value, w_out, ordered, query, keys, values, d_mixed, hidden, masked):
    @pl.when(pl.program_id(0) == 0)
    def _():
        hidden[...] = normalize(frames[...])[0].astype(BF16)
        row = lax.broadcasted_iota(jnp.int32, (ROWS, D), 0) + here()
        masked[...] = jnp.where(row < length[0], grads[...].astype(F32), 0.0).astype(BF16)

    rows = hidden[...]
    now = pair_columns()
    d_mixed[:, now] = dot_nt(masked[...], w_out[...]).astype(BF16)
    query[:, now] = dot(rows, w_query[...]).astype(BF16)
    keys[:, now] = dot(rows, w_key[...]).astype(BF16)
    values[:, now] = dot(rows, w_value[...]).astype(BF16)
    ordered[now] = dot_nt(one_hot(target, pl.program_id(0) * (PAIR // 8), PAIR // 8), rows).astype(BF16)


def front(length, target, frames, grads, w_query, w_key, w_value, w_out):
    wide = jax.ShapeDtypeStruct((ROWS, D), BF16)
    return call(
        front_body,
        [jax.ShapeDtypeStruct((D, ROWS), BF16), wide, wide, wide, wide],
        (length, target, frames, grads, w_query, w_key, w_value, w_out),
        [SCALAR, SCALAR, whole(ROWS, D), whole(ROWS, D)] + [columns(D)] * 3 + [pl.BlockSpec((PAIR, D), lambda j: (j, 0))],
        [HELD] * 5,
        [pltpu.VMEM((ROWS, D), BF16)] * 2,
        5 * ROWS * D * D,
        room=ROOM[0],
    )


def attend_body(
    length, target, low, high, query_all, keys_all, values_all, d_mixed_all, w_key, w_value,
    grad_query_all, grad_key_all, grad_value_all, border_grads_all, ordered_border,
    hidden_border, key_value, pair, score_t, prob_t,
):
    scale = HDIM ** (-0.5)
    blocks = ROWS // WIN

    @pl.when(pl.program_id(0) == 0)
    def _():
        hidden_border[:WIN] = normalize(low[...])[0].astype(BF16)
        hidden_border[WIN:] = normalize(high[...])[0].astype(BF16)
        for part in range(4):
            rows = slice(part * PAIR, (part + 1) * PAIR)
            ordered_border[rows] = dot_nt(one_hot(target, part * (PAIR // 8), PAIR // 8), hidden_border[...]).astype(BF16)
        pair[...] = jnp.zeros_like(pair)
        outside = jnp.zeros((WIN, WIN), BF16)
        for ref in (score_t, prob_t):
            for head in range(2):
                for i in range(0, blocks, 2):
                    ref[head, (i + 3) * WIN : (i + 4) * WIN, i * WIN : (i + 1) * WIN] = outside
                    ref[head, i * WIN : (i + 1) * WIN, (i + 1) * WIN : (i + 2) * WIN] = outside

    query, keys, values, d_mixed = (
        ref.at[:, pair_columns()] for ref in (query_all, keys_all, values_all, d_mixed_all)
    )
    grad_query, grad_key, grad_value = (
        ref.at[:, pair_columns()] for ref in (grad_query_all, grad_key_all, grad_value_all)
    )
    border_grads = border_grads_all.at[:, :, pair_columns()]
    key_border = dot(hidden_border[...], w_key[...]).astype(BF16)
    value_border = dot(hidden_border[...], w_value[...]).astype(BF16)
    above = lax.broadcasted_iota(jnp.int32, (3 * WIN, WIN), 0)
    lane = lax.broadcasted_iota(jnp.int32, (1, WIN), 1)

    def lay_out(head):
        cols = slice(head * HDIM, (head + 1) * HDIM)
        for side, own, to in ((key_border, keys, slice(0, HDIM)), (value_border, values, slice(HDIM, PAIR))):
            key_value[head, :WIN, to] = side[:WIN, cols]
            key_value[head, WIN : WIN + ROWS, to] = own[:, cols]
            key_value[head, WIN + ROWS :, to] = side[WIN:, cols]
        for i in range(blocks):
            mine = slice(i * WIN, (i + 1) * WIN)
            pair[head, i * PAIR : i * PAIR + WIN, :HDIM] = query[mine, cols]
            pair[head, i * PAIR + WIN : (i + 1) * PAIR, HDIM:] = d_mixed[mine, cols]

    def products(head, i):
        return dot_nt(key_value[head, i * WIN : (i + 3) * WIN], pair[head, i * PAIR : (i + 1) * PAIR])

    def soften(head, i, both):
        mine = slice(i * WIN, (i + 1) * WIN)
        reach = slice(i * WIN, (i + 3) * WIN)
        first = (1 - i) * WIN - here()
        last = length[0] - here() + (1 - i) * WIN - 1
        allowed = (above >= jnp.maximum(lane, first)) & (above <= jnp.minimum(lane + 2 * WIN, last))
        scores = jnp.where(allowed, both[:, :WIN], masked_value)
        d_prob = both[:, WIN:]
        row_max = jnp.max(scores, 0, keepdims=True)
        expo = jnp.exp2((scores - row_max) * (scale * math.log2(math.e)))
        inverse_sum = 1.0 / jnp.sum(expo, 0, keepdims=True)
        row_delta = jnp.sum(expo * d_prob, 0, keepdims=True) * inverse_sum
        score_t[head, reach, mine] = (expo * (inverse_sum * scale) * (d_prob - row_delta)).astype(BF16)
        prob_t[head, reach, mine] = (expo * inverse_sum).astype(BF16)

    def query_grads(head, part):
        cols = slice(head * HDIM, (head + 1) * HDIM)
        mine = slice(part * PAIR, (part + 1) * PAIR)
        reach = slice(part * PAIR, part * PAIR + 2 * PAIR)
        grad_query[mine, cols] = dot_tn(score_t[head, reach, mine], key_value[head, reach, :HDIM]).astype(BF16)

    def key_grads(head, part):
        cols = slice(head * HDIM, (head + 1) * HDIM)
        here = slice(part * PAIR, (part + 1) * PAIR)
        near = slice(max(0, part - 1) * PAIR, min(2, part + 1) * PAIR)
        g_key = dot(score_t[head, here, near], query[near, cols]).astype(BF16)
        g_value = dot(prob_t[head, here, near], d_mixed[near, cols]).astype(BF16)
        if part == 0:
            border_grads[0, :WIN, cols], border_grads[1, :WIN, cols] = g_key[:WIN], g_value[:WIN]
            grad_key[:WIN, cols], grad_value[:WIN, cols] = g_key[WIN:], g_value[WIN:]
        elif part == 1:
            grad_key[WIN : WIN + PAIR, cols], grad_value[WIN : WIN + PAIR, cols] = g_key, g_value
        else:
            grad_key[ROWS - WIN :, cols], grad_value[ROWS - WIN :, cols] = g_key[:WIN], g_value[:WIN]
            border_grads[0, WIN:, cols], border_grads[1, WIN:, cols] = g_key[WIN:], g_value[WIN:]

    lay_out(0)
    lay_out(1)
    first = [products(0, i) for i in range(blocks)]
    second = []
    for i in range(blocks):
        soften(0, i, first[i])
        second.append(products(1, i))
        if i == 1:
            query_grads(0, 0)
            key_grads(0, 0)
    for i in range(blocks):
        soften(1, i, second[i])
        if i == 0:
            query_grads(0, 1)
            key_grads(0, 1)
        if i == 1:
            key_grads(0, 2)
            query_grads(1, 0)
            key_grads(1, 0)
    query_grads(1, 1)
    key_grads(1, 1)
    key_grads(1, 2)


def attend(length, target, low, high, query, keys, values, d_mixed, w_key, w_value):
    own = jax.ShapeDtypeStruct((ROWS, D), BF16)
    reach = ROWS + 2 * WIN
    return call(
        attend_body,
        [own] * 3 + [jax.ShapeDtypeStruct((2, 2 * WIN, D), BF16), jax.ShapeDtypeStruct((D, 2 * WIN), BF16)],
        (length, target, low, high, query, keys, values, d_mixed, w_key, w_value),
        [SCALAR, SCALAR, whole(WIN, D), whole(WIN, D)] + [HELD] * 4 + [columns(D)] * 2,
        [HELD] * 5,
        [
            pltpu.VMEM((2 * WIN, D), BF16),
            pltpu.VMEM((2, reach, PAIR), BF16),
            pltpu.VMEM((2, 2 * ROWS, PAIR), BF16),
            pltpu.VMEM((2, reach, ROWS), BF16),
            pltpu.VMEM((2, reach, ROWS), BF16),
        ],
        D * D * WIN * 4 + 10 * 4 * 3 * HEADS * WIN**3,
        room=ROOM[2],
    )


def project_body(ordered, grad, kept, sent):
    half = D // 2
    for now in (slice(j * PAIR, (j + 1) * PAIR) for j in range(STEPS)):
        sent[:, now] = dot(ordered[half:], grad[:, now]).astype(BF16)
        kept[:, now] = dot(ordered[:half], grad[:, now]).astype(BF16)


def project_border_body(part, ordered, grad, ordered_border, border_grads, *rest):
    kept, sent = rest[-2:]
    half = D // 2
    for now in (slice(j * PAIR, (j + 1) * PAIR) for j in range(STEPS)):
        for out, rows in ((sent, slice(half, D)), (kept, slice(0, half))):
            own, border = dot(ordered[rows], grad[:, now]), dot(ordered_border[rows], border_grads[part - 1, :, now])
            out[:, now] = (own + border).astype(BF16)


def project(part, *ins):
    half = jax.ShapeDtypeStruct((D // 2, D), BF16)
    body = functools.partial(project_border_body, part) if part else project_body
    specs = [HELD] * min(len(ins), 4) + [AFTER] * (len(ins) - 4)
    return call(body, [half] * 2, ins, specs, [HELD] * 2, [], D * D * (ROWS + 2 * WIN), steps=1, room=20)


def back_body(grad_query, grad_key, grad_value, w_query, w_key, w_value, *rest):
    total = rest[-1]
    total[:, pair_columns()] = (
        dot_nt(grad_query[...], w_query[...]) + dot_nt(grad_key[...], w_key[...]) + dot_nt(grad_value[...], w_value[...])
    )


def rows_of(columns):
    return pl.BlockSpec((PAIR, columns), lambda j: (j, 0))


def back(*ins):
    return call(
        back_body,
        jax.ShapeDtypeStruct((ROWS, D), F32),
        ins,
        [HELD] * 3 + [rows_of(D)] * 3 + [AFTER] * 3,
        HELD,
        [],
        3 * ROWS * D * D,
        room=24,
    )


def back_border_body(grads, w_key, w_value, *rest):
    sides = rest[-1]
    sides[:, pair_columns()] = (dot_nt(grads[0], w_key[...]) + dot_nt(grads[1], w_value[...])).astype(BF16)


def back_border(*ins):
    return call(
        back_border_body,
        jax.ShapeDtypeStruct((2 * WIN, D), BF16),
        ins,
        [HELD] + [rows_of(D)] * 2 + [AFTER] * 3,
        HELD,
        [],
        4 * WIN * D * D,
        room=16,
    )


def finish_body(frames, grads, d_hidden, near, after, out):
    normed, inverse = normalize(frames[...])
    part = pl.program_id(0)
    inner = jnp.logical_and(part > 0, part < STEPS - 1)
    d_rows = d_hidden[...] + jnp.where(inner, 0.0, near[...].astype(F32))
    mean_grad = jnp.mean(d_rows, -1, keepdims=True)
    mean_cross = jnp.mean(d_rows * normed, -1, keepdims=True)
    out[...] = (grads[...].astype(F32) + inverse * (d_rows - mean_grad - normed * mean_cross)).astype(BF16)


def finish(frames, grads, d_hidden, near, after):
    block = pl.BlockSpec((WIN, D), lambda j: (j, 0))
    return call(
        finish_body,
        jax.ShapeDtypeStruct((ROWS, D), BF16),
        (frames, grads, d_hidden, near, after),
        [block] * 3 + [pl.BlockSpec((WIN, D), lambda j: (j // (STEPS - 1), 0)), AFTER],
        block,
        [],
        ROWS * D * 16,
        room=16,
    )


def swap(first, last, pairs):
    even = lax.axis_index("tm") % 2 == 0
    return send(jnp.where(even, last, first) if pairs == 0 else jnp.where(even, first, last), pairs)


def send(rows, pairs):
    count = lax.axis_size("tm")
    if pairs == 0:
        return lax.ppermute(rows, "tm", [(i, i ^ 1) for i in range(count)])
    return lax.ppermute(rows, "tm", [(i, i + 1 if i % 2 else i - 1) for i in range(1, count - 1)])


def choose_body(sides, *rest):
    within, across = rest[-2:]
    even = lax.axis_index("tm") % 2 == 0

    @pl.when(even)
    def _():
        within[...] = sides[WIN:]
        across[...] = sides[:WIN]

    @pl.when(jnp.logical_not(even))
    def _():
        within[...] = sides[:WIN]
        across[...] = sides[WIN:]


def choose(sides, *after):
    half = jax.ShapeDtypeStruct((WIN, D), BF16)
    return call(choose_body, [half] * 2, (sides, *after), [whole(2 * WIN, D)] + [AFTER] * 3, [whole(WIN, D)] * 2, [], 0, steps=1, room=8)


def in_order(within, across):
    even = lax.axis_index("tm") % 2 == 0
    return jnp.where(even, across, within), jnp.where(even, within, across)


def in_hbm(*arrays):
    return [pltpu.with_memory_space_constraint(array, pltpu.HBM) for array in arrays]


def shards(frames, cotangent, lengths, w_query, w_key, w_value, w_out):
    rows, grads = frames[0], cotangent[0]
    w_query, w_key, w_value, w_out = in_hbm(w_query, w_key, w_value, w_out)
    top, end = rows[:WIN], rows[ROWS - WIN :]
    within, across = swap(top, end, 0), swap(top, end, 1)
    target = block_targets()
    ordered, query, keys, values, d_mixed = front(lengths, target, *in_hbm(rows, grads), w_query, w_key, w_value, w_out)
    low, high = in_order(within, across)
    grad_query, grad_key, grad_value, border_grads, ordered_border = attend(
        lengths, target, low, high, query, keys, values, d_mixed, w_key, w_value
    )
    parts = []
    for part, ins in enumerate(
        (
            (ordered, grad_query),
            (ordered, grad_key, ordered_border, border_grads),
            (ordered, grad_value, ordered_border, border_grads),
        )
    ):
        kept, sent = project(part, *ins, *(parts[0][1:] if part == 2 else ()))
        parts.append(split([kept, exchange(sent, (CORE, CORE))], part))

    def first(after, _):
        d_hidden = back(grad_query, grad_key, grad_value, w_query, w_key, w_value, *after)
        return d_hidden, d_hidden

    def second(after, d_hidden):
        sides = back_border(border_grads, w_key, w_value, *after)
        return (d_hidden, sides), sides

    def third(after, before):
        d_hidden, sides = before
        within, across = choose(sides, *after)
        return (d_hidden, send(within, 0), send(across, 1)), within

    weight_part, (d_hidden, within, across) = scatter_sum(parts, (first, second, third))
    grad_frames = finish(rows, grads, d_hidden, jnp.concatenate(in_order(within, across)), parts[2][1])
    return (grad_frames[None], weight_part)


def solution(mesh):
    placed = (P("rec", "tm", None), P("rec", "tm", None), P("rec"), P(), P(), P(), P())
    return jax.shard_map(
        shards,
        mesh=mesh,
        in_specs=placed,
        out_specs=(P("rec", "tm", None), P(("rec", "tm"), None)),
        check_vma=False,
    )
```
